32 devices in a mesh: pipe: 4 (over y, x), expert: 8 (over z, core).
Axes of the slice: x: 2, y: 2, z: 4, core: 2. Of those that a mesh axis runs over, the one named last changes fastest.
Arguments:
- x_fwd: bfloat16 [4096, 1536], P(('pipe', 'expert')), may hold values from -6 to 6
- gate_fwd: float32 [4096, 6], P(('pipe', 'expert')), may hold values from 0.05 to 0.4
- route_fwd: int32 [4096, 6], P(('pipe', 'expert')), may hold values from 0 to 15, all different within a row; in each aligned block of 128 rows (0 to 127, 128 to 255, ...) at most 64 rows name the same one
- x_bwd: bfloat16 [4096, 1536], P(('pipe', 'expert')), may hold values from -6 to 6
- gate_bwd: float32 [4096, 6], P(('pipe', 'expert')), may hold values from 0.05 to 0.4
- route_bwd: int32 [4096, 6], P(('pipe', 'expert')), may hold values from 0 to 15, all different within a row; in each aligned block of 128 rows (0 to 127, 128 to 255, ...) at most 64 rows name the same one
- cotangent: bfloat16 [4096, 1536], P(('pipe', 'expert')), may hold values from -6 to 6
- norm_gain: float32 [1536], replicated, may hold values from 0.5 to 1.5
- w_gate_up: bfloat16 [4, 16, 1536, 1536], P('pipe', 'expert'), as said below
- w_down: bfloat16 [4, 16, 768, 1536], P('pipe', 'expert'), as said below
Outputs:
- y_fwd: bfloat16 [4096, 1536], P(('pipe', 'expert'))
- dx_bwd: bfloat16 [4096, 1536], P(('pipe', 'expert'))
- grad_gate_up: bfloat16 [4, 8, 1536, 1536], P('pipe', 'expert')
- grad_down: bfloat16 [4, 8, 768, 1536], P('pipe', 'expert')
The draws below stay inside these ranges and needn't reach their ends.
Inputs may be any that keep to these rules, and one draw needn't show every extreme that they name: `route_fwd`: each row names 6 different experts; in the 128 rows of one group no expert is named more than 64 times. `route_bwd`: each row names 6 different experts; in the 128 rows of one group no expert is named more than 64 times. w_gate_up[p] equals w_gate_up[3 - p]. w_down[p] equals w_down[3 - p].
All inputs are finite; a program needn't handle non-finite values.
Results may differ from the reference program's by a relative error of at most 0.0078.
Values may be sent and summed in bfloat16 or wider, within the bound.
No kernel may reach another device: no remote copies, remote signals or barrier semaphores. Data moves between devices by JAX's collectives and lax.ppermute only.
A program may use at most 192 MiB of HBM per device.

```python
import math
import jax
import jax.numpy as jnp
import numpy as np
from jax import lax

D = 1536
FF = 768
TOP = 6
EXP_DEV = 2
TOK_DEV = 128
SECTIONS = 4
GROUPS = 8
EXPERTS = 16
CAP = 64
ROWS = 4096


def mirrored_weights(key, shape, fan_in):
    half_shape = (SECTIONS // 2,) + shape
    values = jax.random.normal(key, half_shape, jnp.float32)
    values = (values * fan_in ** (-0.5)).astype(jnp.bfloat16)
    return jnp.concatenate([values, values[::-1]], axis=0)


def draw_w_gate_up(key, part):
    return mirrored_weights(jax.random.fold_in(key, 11), (EXPERTS, D, 2 * FF), D)


def draw_w_down(key, part):
    return mirrored_weights(jax.random.fold_in(key, 23), (EXPERTS, FF, D), FF)


def block_scale(key, dims, split, low, top_value):
    def one(position, shards_of):
        draws = jax.random.uniform(jax.random.fold_in(jax.random.fold_in(key, 6), position), (shards_of,), jnp.float32, low / len(split), top_value / len(split))
        return jnp.repeat(jnp.exp(draws), dims[position] // shards_of).reshape((-1,) + (1,) * (len(dims) - position - 1))

    factor_of = one(*split[0])
    for cut in split[1:]:
        factor_of = factor_of * one(*cut)
    return factor_of


def shared_out(own_key, own, number, rows, number_of, top, most, skew):
    order = jax.random.permutation(own_key, number_of)
    packed, ordinary = load_shares(number_of, rows * top, most, skew, True), load_shares(number_of, rows * top, most, skew, False)
    places = jnp.arange(number_of)

    def named(tallies, rotation):
        used = int((tallies > 0).sum())
        fixed = max(1, used // 4)
        passed = fixed + (places - fixed + rotation * (used - fixed)) % max(1, number_of - fixed)
        return jnp.zeros((number_of,), jnp.int32).at[order[jnp.where(places < fixed, places, passed)]].set(jnp.asarray(tallies, jnp.int32))

    tallies = jnp.where(number % 4 == 0, named(packed, number // 4), named(ordinary, number - number // 4 - 1))
    mixed = jax.random.permutation(jax.random.fold_in(own, 3), number_of)
    source_of, sink = mixed[0:number_of // 2 * 2:2], mixed[1:number_of // 2 * 2:2]
    room = jnp.minimum(tallies[source_of] - 1, most - tallies[sink]) // 2
    room = jnp.where((source_of == order[0]) | (sink == order[0]) | (tallies[sink] == 0), 0, jnp.maximum(room, 0))
    passed = jax.random.randint(jax.random.fold_in(own, 4), (number_of // 2,), 0, 1 << 20) % (room + 1)
    tallies = tallies.at[source_of].add(-passed).at[sink].add(passed)
    members = jnp.searchsorted(jnp.cumsum(tallies), jnp.arange(rows * top), side="right").astype(jnp.int32)
    table = members.reshape(top, rows).T
    table = table[jax.random.permutation(jax.random.fold_in(own, 1), rows)]
    rotation = jax.random.randint(jax.random.fold_in(own, 2), (rows, 1), 0, top)
    return jnp.take_along_axis(table, (jnp.arange(top)[None, :] + rotation) % top, axis=1)


def load_shares(amount, total, limit, skew, full):
    portions = [(1 << 20) // math.isqrt(standing ** skew) + 1 for standing in range(1, amount + 1)]
    largest = limit if full else min(limit, max(-(-total // amount), total * portions[0] // sum(portions)))
    least = 1 if total - largest >= amount - 1 else 0
    counts, spare = [largest] + [least] * (amount - 1), total - largest - least * (amount - 1)
    while spare > 0:
        movable = [i for i in range(1, amount) if counts[i] < largest] or [i for i in range(1, amount) if counts[i] < limit]
        whole, left = sum([portions[i] for i in movable]), spare
        for i in movable:
            extra = min(limit - counts[i], max(1, left * portions[i] // whole), spare)
            counts[i] = counts[i] + extra
            spare = spare - extra
    return np.array(counts)


def gaussian(key, dims, scale, reach, shards=(), kind=jnp.bfloat16):
    loudness = block_scale(key, dims, shards, -0.22, 0.18) if shards else 1.0
    drawn = jax.random.normal(key, dims, jnp.float32) * scale * loudness
    return jnp.minimum(jnp.maximum(drawn, -reach), reach).astype(kind)


def setup_inputs(seed: int = 0) -> dict:
    seeds = jax.random.split(jax.random.key(seed), 11)
    x_fwd = gaussian(seeds[0], (ROWS, D), 1.0, 6.0, ((0, 32),))
    gate_fwd = jnp.clip(0.05 + 0.35 * jax.random.uniform(seeds[1], (ROWS, TOP), jnp.float32) ** block_scale(seeds[1], (ROWS, TOP), ((0, 32),), -0.2, 0.2), 0.05, 0.4)
    route_fwd_keys = jax.random.split(jax.random.fold_in(seeds[2], 1), ROWS // TOK_DEV)
    route_fwd_turns = jax.random.permutation(jax.random.fold_in(seeds[2], 3), ROWS // TOK_DEV)
    route_fwd = jax.vmap(lambda own, number: shared_out(jax.random.fold_in(seeds[2], 2), own, number, TOK_DEV, EXPERTS, TOP, CAP, 2))(route_fwd_keys, route_fwd_turns).reshape((ROWS, TOP))
    x_bwd = gaussian(seeds[3], (ROWS, D), 1.0, 6.0, ((0, 32),))
    gate_bwd = jnp.clip(0.05 + 0.35 * jax.random.uniform(seeds[4], (ROWS, TOP), jnp.float32) ** block_scale(seeds[4], (ROWS, TOP), ((0, 32),), -0.2, 0.2), 0.05, 0.4)
    route_bwd_keys = jax.random.split(jax.random.fold_in(seeds[5], 1), ROWS // TOK_DEV)
    route_bwd_turns = jax.random.permutation(jax.random.fold_in(seeds[5], 3), ROWS // TOK_DEV)
    route_bwd = jax.vmap(lambda own, number: shared_out(jax.random.fold_in(seeds[5], 2), own, number, TOK_DEV, EXPERTS, TOP, CAP, 2))(route_bwd_keys, route_bwd_turns).reshape((ROWS, TOP))
    cotangent = gaussian(seeds[6], (ROWS, D), 1.0, 6.0, ((0, 32),))
    norm_gain = jnp.clip(1.0 + 0.1 * jax.random.normal(seeds[7], (D,), jnp.float32), 0.5, 1.5)
    w_gate_up = draw_w_gate_up(jax.random.fold_in(seeds[10], 71), 0)
    w_down = draw_w_down(jax.random.fold_in(seeds[10], 71), 0)
    return dict(x_fwd=x_fwd, gate_fwd=gate_fwd, route_fwd=route_fwd, x_bwd=x_bwd, gate_bwd=gate_bwd, route_bwd=route_bwd, cotangent=cotangent, norm_gain=norm_gain, w_gate_up=w_gate_up, w_down=w_down)


norm_eps = 1e-06

def normalize(inputs):
    values = inputs.astype(jnp.float32)
    scale = lax.rsqrt(lax.optimization_barrier(jnp.mean(values * values, axis=-1, keepdims=True)) + norm_eps)
    return (values * scale, scale)

def destinations(routes, expert_count, capacity):
    flat_routes = routes.reshape(-1)
    onehot = (flat_routes[:, None] == jnp.arange(expert_count, dtype=jnp.int32)[None, :]).astype(jnp.int32)
    before = jnp.cumsum(onehot, axis=0) - onehot
    slot = lax.optimization_barrier(jnp.sum(before * onehot, axis=1))
    return (flat_routes * capacity + slot).astype(jnp.int32).reshape(routes.shape)

def expert_forward(inputs, weight_gu, weight_dn):
    hidden_units = weight_dn.shape[1]
    both_parts = jnp.einsum('secd,edf->secf', inputs.astype(jnp.float32), weight_gu.astype(jnp.float32))
    gate_pre = both_parts[..., :hidden_units]
    up_pre = both_parts[..., hidden_units:]
    hidden = (jax.nn.silu(gate_pre) * up_pre).astype(jnp.bfloat16)
    return jnp.einsum('secf,efd->secd', hidden.astype(jnp.float32), weight_dn.astype(jnp.float32)).astype(jnp.bfloat16)

def expert_backward(inputs, cot_rows, weight_gu, weight_dn):
    hidden_units = weight_dn.shape[1]
    inputs_f = inputs.astype(jnp.float32)
    cot_f = cot_rows.astype(jnp.float32)
    gu_f = weight_gu.astype(jnp.float32)
    both_parts = jnp.einsum('secd,edf->secf', inputs_f, gu_f)
    gate_pre = both_parts[..., :hidden_units]
    up_pre = both_parts[..., hidden_units:]
    squash = jax.nn.sigmoid(gate_pre)
    activated = gate_pre * squash
    hidden = (activated * up_pre).astype(jnp.bfloat16)
    back_hidden = jnp.einsum('secd,efd->secf', cot_f, weight_dn.astype(jnp.float32))
    d_gate = back_hidden * up_pre * squash * (1.0 + gate_pre * (1.0 - squash))
    d_up = back_hidden * activated
    d_both = jnp.concatenate([d_gate, d_up], axis=-1).astype(jnp.bfloat16)
    d_both_f = d_both.astype(jnp.float32)
    d_inputs = jnp.einsum('secf,edf->secd', d_both_f, gu_f).astype(jnp.bfloat16)
    grad_dn = jnp.einsum('secf,secd->efd', hidden.astype(jnp.float32), cot_f).astype(jnp.bfloat16)
    grad_gu = jnp.einsum('secd,secf->edf', inputs_f, d_both_f).astype(jnp.bfloat16)
    return (d_inputs, grad_gu, grad_dn)

def rank_pass(x_f, g_f, r_f, x_b, g_b, r_b, cot, gain, weight_gu, weight_dn):
    slot_total = EXPERTS * CAP
    buffer_shape = (GROUPS, EXPERTS, CAP, D)

    def dest_of(routes):
        return destinations(routes, EXPERTS, CAP)

    def place_rows(values, dest):
        flat_values = values.reshape(-1, values.shape[-1])
        return jnp.zeros((slot_total, values.shape[-1]), values.dtype).at[dest.reshape(-1)].set(flat_values)

    def pick_rows(back, dest):
        return back[dest]
    h_f = (normalize(x_f)[0] * gain).astype(jnp.bfloat16)
    dest_f = jax.vmap(dest_of)(r_f)
    rows_f = jnp.broadcast_to(h_f[:, :, None, :], (GROUPS, TOK_DEV, TOP, D))
    send_f = jax.vmap(place_rows)(rows_f, dest_f).reshape(buffer_shape)
    out_f = expert_forward(send_f, weight_gu, weight_dn).reshape(GROUPS, slot_total, D)
    picked = jax.vmap(pick_rows)(out_f, dest_f)
    y_rows = lax.optimization_barrier(jnp.sum(picked.astype(jnp.float32) * g_f[..., None], axis=2)).astype(jnp.bfloat16)
    x_hat, scale = normalize(x_b)
    h_b = (x_hat * gain).astype(jnp.bfloat16)
    c_b = (g_b[..., None] * cot.astype(jnp.float32)[:, :, None, :]).astype(jnp.bfloat16)
    dest_b = jax.vmap(dest_of)(r_b)
    rows_b = jnp.broadcast_to(h_b[:, :, None, :], (GROUPS, TOK_DEV, TOP, D))
    send_h = jax.vmap(place_rows)(rows_b, dest_b).reshape(buffer_shape)
    send_c = jax.vmap(place_rows)(c_b, dest_b).reshape(buffer_shape)
    d_inputs, grad_gu, grad_dn = expert_backward(send_h, send_c, weight_gu, weight_dn)
    back_dh = d_inputs.reshape(GROUPS, slot_total, D)
    dh_sum = lax.optimization_barrier(jnp.sum(jax.vmap(pick_rows)(back_dh, dest_b).astype(jnp.float32), axis=2))
    scaled_dh = gain * dh_sum
    dx_rows = (scale * (scaled_dh - x_hat * lax.optimization_barrier(jnp.mean(x_hat * scaled_dh, axis=-1, keepdims=True)))).astype(jnp.bfloat16)
    return (y_rows, dx_rows, grad_gu, grad_dn)

def reference(x_fwd, gate_fwd, route_fwd, x_bwd, gate_bwd, route_bwd, cotangent, norm_gain, w_gate_up, w_down):
    stacked = (x_fwd.reshape(SECTIONS, GROUPS, TOK_DEV, D), gate_fwd.reshape(SECTIONS, GROUPS, TOK_DEV, TOP), route_fwd.reshape(SECTIONS, GROUPS, TOK_DEV, TOP), x_bwd.reshape(SECTIONS, GROUPS, TOK_DEV, D), gate_bwd.reshape(SECTIONS, GROUPS, TOK_DEV, TOP), route_bwd.reshape(SECTIONS, GROUPS, TOK_DEV, TOP), cotangent.reshape(SECTIONS, GROUPS, TOK_DEV, D))
    half_local = EXP_DEV // 2

    def take_row(array, index):
        return lax.dynamic_index_in_dim(array, index, 0, keepdims=False)

    def run_rank(index):
        pieces = [take_row(array, index) for array in stacked]
        return rank_pass(*pieces, norm_gain, take_row(w_gate_up, index), take_row(w_down, index))

    def pair_pass(lower):
        mirror = (SECTIONS - 1 - lower).astype(jnp.int32)
        low_side = run_rank(lower)
        high_side = run_rank(mirror)
        sum_gu = (low_side[2].astype(jnp.float32) + high_side[2].astype(jnp.float32)).astype(jnp.bfloat16)
        sum_dn = (low_side[3].astype(jnp.float32) + high_side[3].astype(jnp.float32)).astype(jnp.bfloat16)
        sum_gu = sum_gu.reshape(GROUPS, EXP_DEV, D, 2 * FF)
        sum_dn = sum_dn.reshape(GROUPS, EXP_DEV, FF, D)
        return (low_side[0], low_side[1], high_side[0], high_side[1], sum_gu[:, :half_local].reshape(GROUPS * half_local, D, 2 * FF), sum_gu[:, half_local:].reshape(GROUPS * half_local, D, 2 * FF), sum_dn[:, :half_local].reshape(GROUPS * half_local, FF, D), sum_dn[:, half_local:].reshape(GROUPS * half_local, FF, D))
    results = lax.map(pair_pass, jnp.arange(SECTIONS // 2, dtype=jnp.int32))
    y_fwd = jnp.concatenate([results[0], results[2][::-1]], axis=0).reshape(ROWS, D)
    dx_bwd = jnp.concatenate([results[1], results[3][::-1]], axis=0).reshape(ROWS, D)
    grad_gate_up = jnp.concatenate([results[4], results[5][::-1]], axis=0)
    grad_down = jnp.concatenate([results[6], results[7][::-1]], axis=0)
    return (y_fwd, dx_bwd, grad_gate_up, grad_down)
```

```python
import jax
import jax.numpy as jnp
from jax import lax
from jax.sharding import PartitionSpec as P

norm_eps = 1e-06


def normalize(inputs):
    values = inputs.astype(jnp.float32)
    scale = lax.rsqrt(jnp.mean(values * values, axis=-1, keepdims=True) + norm_eps)
    return (values * scale, scale)


def expert_gates(gates, routes, expert_count):
    chosen = routes[None, :, :] == jnp.arange(expert_count, dtype=jnp.int32)[:, None, None]
    return jnp.sum(jnp.where(chosen, gates[None], 0.0), axis=-1)


def placement(gates, capacity):
    named = gates > 0.0
    slot = jnp.cumsum(named.astype(jnp.int32), axis=-1) - 1
    wanted = jnp.arange(capacity, dtype=jnp.int32)[:, None]
    onehot = (slot[..., None, :] == wanted) & named[..., None, :]
    slot_gates = jnp.sum(jnp.where(onehot, gates[..., None, :], 0.0), axis=-1)
    return (onehot.astype(jnp.bfloat16), slot_gates)


def hidden_parts(inputs, weight_gu, hidden_units):
    both_parts = jnp.einsum("erd,edf->erf", inputs, weight_gu, preferred_element_type=jnp.float32)
    return (both_parts[..., :hidden_units], both_parts[..., hidden_units:])


def backward_parts(inputs, cot_rows, weight_gu, weight_dn):
    gate_pre, up_pre = hidden_parts(inputs, weight_gu, weight_dn.shape[1])
    squash = jax.nn.sigmoid(gate_pre)
    activated = gate_pre * squash
    hidden = (activated * up_pre).astype(jnp.bfloat16)
    back_hidden = jnp.einsum(
        "erd,efd->erf", cot_rows, weight_dn, preferred_element_type=jnp.float32
    )
    d_gate = back_hidden * up_pre * squash * (1.0 + gate_pre * (1.0 - squash))
    d_up = back_hidden * activated
    return (hidden, jnp.concatenate([d_gate, d_up], axis=-1).astype(jnp.bfloat16))


def per_device(
    x_fwd, gate_fwd, route_fwd, x_bwd, gate_bwd, route_bwd, cotangent, norm_gain, w_gate_up, w_down
):
    group_count = lax.axis_size("expert")
    section_count = lax.axis_size("pipe")
    local_count = w_gate_up.shape[1]
    expert_count = local_count * group_count
    token_count, model_width = x_fwd.shape
    pick_count = route_fwd.shape[1]
    capacity = token_count * pick_count * 4 // (3 * expert_count)
    row_count = group_count * capacity
    weight_gu = w_gate_up[0]
    weight_dn = w_down[0]
    hidden_units = weight_dn.shape[1]

    bwd_hat, bwd_scale = normalize(x_bwd)
    bwd_normed = (bwd_hat * norm_gain).astype(jnp.bfloat16)
    fwd_normed = (normalize(x_fwd)[0] * norm_gain).astype(jnp.bfloat16)

    send_gates = jnp.stack(
        [
            expert_gates(gate_fwd, route_fwd, expert_count),
            expert_gates(gate_bwd, route_bwd, expert_count),
        ]
    ).reshape(2, group_count, local_count, token_count)
    recv_gates = lax.all_to_all(
        send_gates.transpose(1, 0, 2, 3), "expert", split_axis=0, concat_axis=0, tiled=True
    ).transpose(1, 2, 0, 3)

    gathered_bwd = lax.all_gather(
        jnp.concatenate([bwd_normed, cotangent], axis=0)[None], "expert", axis=0, tiled=True
    )
    gathered_fwd = lax.all_gather(fwd_normed[None], "expert", axis=0, tiled=True)

    place_bwd, slot_gates_bwd = placement(recv_gates[1], capacity)
    rows_h = jnp.einsum(
        "egst,gtd->egsd", place_bwd, gathered_bwd[:, :token_count], preferred_element_type=jnp.float32
    ).astype(jnp.bfloat16)
    rows_c = jnp.einsum(
        "egst,gtd->egsd", place_bwd, gathered_bwd[:, token_count:], preferred_element_type=jnp.float32
    )
    rows_c = (rows_c * slot_gates_bwd[..., None]).astype(jnp.bfloat16)
    rows_h = rows_h.reshape(local_count, row_count, model_width)
    rows_c = rows_c.reshape(local_count, row_count, model_width)

    section_index = lax.axis_index("pipe")
    upper_half = (section_index >= section_count // 2).astype(jnp.int32)
    half_local = local_count // 2

    def kept(value):
        return lax.dynamic_slice_in_dim(value, upper_half * half_local, half_local, 0)

    def given(value):
        return lax.dynamic_slice_in_dim(value, (1 - upper_half) * half_local, half_local, 0)

    mirror = [(i, section_count - 1 - i) for i in range(section_count)]
    mirror_h = lax.ppermute(given(rows_h), "pipe", mirror)
    mirror_c = lax.ppermute(given(rows_c), "pipe", mirror)

    hidden, d_both = backward_parts(rows_h, rows_c, weight_gu, weight_dn)
    d_inputs = jnp.einsum(
        "erf,edf->erd", d_both, weight_gu, preferred_element_type=jnp.float32
    ).astype(jnp.bfloat16)
    partial_dh = jnp.einsum(
        "egst,egsd->gtd",
        place_bwd,
        d_inputs.reshape(local_count, group_count, capacity, model_width),
        preferred_element_type=jnp.float32,
    ).astype(jnp.bfloat16)
    dh_sum = lax.psum_scatter(
        partial_dh.reshape(group_count * token_count, model_width),
        "expert",
        scatter_dimension=0,
        tiled=True,
    ).astype(jnp.float32)

    place_fwd, slot_gates_fwd = placement(recv_gates[0], capacity)
    rows_f = (
        jnp.einsum(
            "egst,gtd->egsd", place_fwd, gathered_fwd, preferred_element_type=jnp.float32
        )
        .astype(jnp.bfloat16)
        .reshape(local_count, row_count, model_width)
    )
    gate_pre, up_pre = hidden_parts(rows_f, weight_gu, hidden_units)
    hidden_fwd = (jax.nn.silu(gate_pre) * up_pre).astype(jnp.bfloat16)
    out_rows = jnp.einsum(
        "erf,efd->erd", hidden_fwd, weight_dn, preferred_element_type=jnp.float32
    )
    out_rows = (out_rows * slot_gates_fwd.reshape(local_count, row_count, 1)).astype(jnp.bfloat16)
    partial_y = jnp.einsum(
        "egst,egsd->gtd",
        place_fwd,
        out_rows.reshape(local_count, group_count, capacity, model_width),
        preferred_element_type=jnp.float32,
    ).astype(jnp.bfloat16)
    y_fwd = lax.psum_scatter(
        partial_y.reshape(group_count * token_count, model_width),
        "expert",
        scatter_dimension=0,
        tiled=True,
    )

    mirror_hidden, mirror_d = backward_parts(mirror_h, mirror_c, kept(weight_gu), kept(weight_dn))
    all_h = jnp.concatenate([kept(rows_h), mirror_h], axis=1)
    all_c = jnp.concatenate([kept(rows_c), mirror_c], axis=1)
    all_hidden = jnp.concatenate([kept(hidden), mirror_hidden], axis=1)
    all_d = jnp.concatenate([kept(d_both), mirror_d], axis=1)
    out_dn = jnp.einsum(
        "erf,erd->efd", all_hidden, all_c, preferred_element_type=jnp.float32
    ).astype(jnp.bfloat16)
    out_gu = jnp.einsum("erd,erf->edf", all_h, all_d, preferred_element_type=jnp.float32).astype(
        jnp.bfloat16
    )

    scaled_dh = norm_gain * dh_sum
    dx_bwd = (
        bwd_scale * (scaled_dh - bwd_hat * jnp.mean(bwd_hat * scaled_dh, axis=-1, keepdims=True))
    ).astype(jnp.bfloat16)
    return (y_fwd, dx_bwd, out_gu[None], out_dn[None])


def solution(mesh):
    rows = P(("pipe", "expert"), None)
    experts = P("pipe", "expert", None, None)
    return jax.shard_map(
        per_device,
        mesh=mesh,
        in_specs=(rows,) * 7 + (P(), experts, experts),
        out_specs=(rows, rows, experts, experts),
        check_vma=False,
    )
```

```python
import functools

import jax
import jax.numpy as jnp
from jax import lax
from jax.experimental import pallas as pl
from jax.experimental.pallas import tpu as pltpu
from jax.sharding import PartitionSpec as P

norm_eps = 1e-06
tile = 256
vmem_bytes = 56 * 1024 * 1024


def params():
    return pltpu.CompilerParams(
        dimension_semantics=("arbitrary",), vmem_limit_bytes=vmem_bytes
    )


def light():
    return pl.CostEstimate(flops=1000, bytes_accessed=1000, transcendentals=0)


def dot(a, b, contract=((1,), (0,))):
    return lax.dot_general(a, b, (contract, ((), ())), preferred_element_type=jnp.float32)


def normalize(inputs):
    values = inputs.astype(jnp.float32)
    scale = lax.rsqrt(jnp.mean(values * values, axis=-1, keepdims=True) + norm_eps)
    return (values * scale, scale)


def expert_gates(gates, routes, expert_count):
    chosen = routes[None, :, :] == jnp.arange(expert_count, dtype=jnp.int32)[:, None, None]
    return jnp.sum(jnp.where(chosen, gates[None], 0.0), axis=-1)


def ranks(gates):
    named = gates > 0.0
    token_count = gates.shape[1]
    upto = lax.broadcasted_iota(jnp.int32, (token_count, token_count), 0) <= (
        lax.broadcasted_iota(jnp.int32, (token_count, token_count), 1)
    )
    count = dot(
        jnp.where(named, 1.0, 0.0).astype(jnp.bfloat16), jnp.where(upto, 1.0, 0.0).astype(jnp.bfloat16)
    )
    return jnp.where(named, count - 1.0, -1.0)


def onehot_rows(rank, group, local_count, capacity):
    token_count = rank.shape[1]
    slots = lax.broadcasted_iota(jnp.int32, (capacity, token_count), 0).astype(jnp.float32)
    parts = []
    for local in range(local_count):
        row = group * local_count + local
        parts.append(jnp.where(rank[row : row + 1, :] == slots, 1.0, 0.0))
    return jnp.concatenate(parts, axis=0)


def slot_gates(onehot, gates, group, local_count, capacity):
    parts = []
    for local in range(local_count):
        row = group * local_count + local
        own = onehot[local * capacity : (local + 1) * capacity]
        parts.append(jnp.sum(own * gates[row : row + 1, :], axis=1, keepdims=True))
    return jnp.concatenate(parts, axis=0)


def cuts(row_count):
    ends = [0, row_count * 5 // 8, row_count * 21 // 16, row_count * 2]
    return [(start, end) for start, end in zip(ends[:-1], ends[1:])]


def overlaps(row_count, start, end):
    for send, (low, high) in enumerate(cuts(row_count)):
        first, last = max(start, low), min(end, high)
        if first < last:
            yield send, slice(first - low, last - low), slice(first - start, last - start)


def place_kernel(
    capacity, sides_ref, c_ref, h_ref, gates_ref, rows_c_ref, rows_h_ref, *give_refs
):
    half = h_ref.shape[0]
    local_count = rows_h_ref.shape[0]
    row_count = 2 * half * capacity

    def place(side):
        gates = gates_ref[0]
        rank = ranks(gates)
        for group in range(half):
            onehot = onehot_rows(rank, group, local_count, capacity)
            scale = slot_gates(onehot, gates, group, local_count, capacity)
            onehot = onehot.astype(jnp.bfloat16)
            rows_c = (dot(onehot, c_ref[group, 0, 0]) * scale).astype(jnp.bfloat16)
            rows_h = dot(onehot, h_ref[group, 0, 0]).astype(jnp.bfloat16)
            for local in range(local_count):
                own = slice(local * capacity, (local + 1) * capacity)
                here = slice(group * capacity, (group + 1) * capacity)
                rows_c_ref[local, here] = rows_c[own]
                rows_h_ref[local, here] = rows_h[own]
            first = (side * half + group) * capacity
            for base, rows in ((first, rows_c), (row_count + first, rows_h)):
                for send, there, part in overlaps(row_count, base, base + capacity):
                    give_refs[send][there] = rows[part]

    for side in range(2):
        pl.when(pl.program_id(0) == side)(functools.partial(place, side))


def place_rows(tokens, gates, sides, capacity):
    group_count, _, token_count, width = tokens.shape
    local_count = gates.shape[1]
    half = group_count // 2
    row_count = group_count * capacity
    rows_spec = pl.BlockSpec((local_count, row_count // 2, width), lambda i, sides: (0, i, 0))
    give_shapes = [(end - start, width) for start, end in cuts(row_count)]
    block = (half, 1, 1, token_count, width)
    tokens = tokens.reshape(half, 2, 2, token_count, width)
    return pl.pallas_call(
        functools.partial(place_kernel, capacity),
        grid_spec=pltpu.PrefetchScalarGridSpec(
            num_scalar_prefetch=1,
            grid=(2,),
            in_specs=[
                pl.BlockSpec(block, lambda i, sides: (0, sides[i], 0, 0, 0)),
                pl.BlockSpec(block, lambda i, sides: (0, sides[i], 1, 0, 0)),
                pl.BlockSpec((1, half * local_count, token_count), lambda i, sides: (i, 0, 0)),
            ],
            out_specs=[rows_spec, rows_spec]
            + [pl.BlockSpec(shape, lambda i, sides: (0, 0)) for shape in give_shapes],
        ),
        out_shape=[jax.ShapeDtypeStruct((local_count, row_count, width), jnp.bfloat16)] * 2
        + [jax.ShapeDtypeStruct(shape, jnp.bfloat16) for shape in give_shapes],
        compiler_params=params(),
        cost_estimate=light(),
        name="place_rows",
    )(sides, tokens, tokens, gates.reshape(2, half * local_count, token_count))


def combine(gates, rows_ref, capacity, local_count, store):
    rank = ranks(gates)
    for group in range(rows_ref.shape[0]):
        onehot = onehot_rows(rank, group, local_count, capacity).T.astype(jnp.bfloat16)
        store(group, dot(onehot, rows_ref[group]).astype(jnp.bfloat16))


def hidden_gradients(h, c, gu_ref, dn_ref, hidden_ref, d_ref):
    hidden_units = dn_ref.shape[1]
    for start in range(0, hidden_units, tile):
        cols = slice(start, start + tile)
        up_cols = slice(hidden_units + start, hidden_units + start + tile)
        gate_pre = dot(h, gu_ref[0, :, cols])
        up_pre = dot(h, gu_ref[0, :, up_cols])
        back = dot(c, dn_ref[0, cols, :], ((1,), (1,)))
        squash = 1.0 / (1.0 + jnp.exp(-gate_pre))
        activated = gate_pre * squash
        hidden_ref[:, cols] = (activated * up_pre).astype(jnp.bfloat16)
        d_ref[:, cols] = (back * up_pre * squash * (1.0 + gate_pre * (1.0 - squash))).astype(
            jnp.bfloat16
        )
        d_ref[:, up_cols] = (back * activated).astype(jnp.bfloat16)


def backward_kernel(
    capacity, which_ref, h_ref, c_ref, gu_ref, dn_ref, gates_ref,
    own_ref, other_ref, hidden_ref, d_ref, dh_ref,
):
    step = pl.program_id(0)
    hidden_units = dn_ref.shape[1]
    width = dn_ref.shape[2]
    group_count = dh_ref.shape[0]
    local_count = dh_ref.shape[1] // capacity
    token_count = gates_ref.shape[1]
    hidden_gradients(h_ref[0], c_ref[0], gu_ref, dn_ref, hidden_ref, d_ref)
    d = d_ref[...]
    for start in range(0, width, tile):
        cols = slice(start, start + tile)
        dh = dot(d, gu_ref[0, cols, :], ((1,), (1,))).astype(jnp.bfloat16)
        dh = dh.reshape(group_count, capacity, tile)
        dh_ref[:, pl.ds(pl.multiple_of(step * capacity, capacity), capacity), cols] = dh

    @pl.when(step == local_count - 1)
    def _():
        half = group_count // 2

        def store(group, value):
            target = own_ref if group < half else other_ref
            target[group % half] = value

        combine(gates_ref[...], dh_ref, capacity, local_count, store)


def backward_rows(rows_h, rows_c, weight_gu, weight_dn, gates, which, capacity):
    local_count, row_count, width = rows_h.shape
    hidden_units = weight_dn.shape[1]
    group_count = row_count // capacity
    token_count = gates.shape[-1]
    half = (group_count // 2, token_count, width)
    whole = lambda shape: pl.BlockSpec(shape, lambda e, which: (0,) * len(shape))
    rows_spec = pl.BlockSpec((1, row_count, width), lambda e, which: (e, 0, 0))
    return pl.pallas_call(
        functools.partial(backward_kernel, capacity),
        grid_spec=pltpu.PrefetchScalarGridSpec(
            num_scalar_prefetch=1,
            grid=(local_count,),
            in_specs=[
                rows_spec,
                rows_spec,
                pl.BlockSpec((1, width, 2 * hidden_units), lambda e, which: (which[e], 0, 0)),
                pl.BlockSpec((1, hidden_units, width), lambda e, which: (which[e], 0, 0)),
                whole((group_count * local_count, token_count)),
            ],
            out_specs=[
                whole(half),
                whole(half),
                whole((row_count, hidden_units)),
                whole((row_count, 2 * hidden_units)),
            ],
            scratch_shapes=[
                pltpu.VMEM((group_count, local_count * capacity, width), jnp.bfloat16)
            ],
        ),
        out_shape=[
            jax.ShapeDtypeStruct(half, jnp.bfloat16),
            jax.ShapeDtypeStruct(half, jnp.bfloat16),
            jax.ShapeDtypeStruct((row_count, hidden_units), jnp.bfloat16),
            jax.ShapeDtypeStruct((row_count, 2 * hidden_units), jnp.bfloat16),
        ],
        compiler_params=params(),
        cost_estimate=light(),
        name="backward_rows",
    )(which, rows_h, rows_c, weight_gu, weight_dn, gates.reshape(-1, token_count))


def forward_kernel(
    capacity, tokens_ref, gates_ref, gu_ref, dn_ref, out_ref, rows_ref, scale_ref, hidden_ref, o_ref
):
    step = pl.program_id(0)
    hidden_units = dn_ref.shape[1]
    width = dn_ref.shape[2]
    group_count = rows_ref.shape[0]
    local_count = rows_ref.shape[1] // capacity
    row_count = group_count * capacity
    own = pl.ds(pl.multiple_of(step * capacity, capacity), capacity)

    @pl.when(step == 0)
    def _():
        gates = gates_ref[...]
        rank = ranks(gates)
        for group in range(group_count):
            onehot = onehot_rows(rank, group, local_count, capacity)
            rows_ref[group] = dot(onehot.astype(jnp.bfloat16), tokens_ref[group]).astype(
                jnp.bfloat16
            )
            scale_ref[group] = jnp.broadcast_to(
                slot_gates(onehot, gates, group, local_count, capacity), scale_ref.shape[1:]
            )

    h = rows_ref[:, own, :].reshape(row_count, width)
    scale = scale_ref[:, own, :].reshape(row_count, scale_ref.shape[2])[:, :1]
    for start in range(0, hidden_units, tile):
        cols = slice(start, start + tile)
        up_cols = slice(hidden_units + start, hidden_units + start + tile)
        gate_pre = dot(h, gu_ref[0, :, cols])
        up_pre = dot(h, gu_ref[0, :, up_cols])
        hidden_ref[:, cols] = (gate_pre / (1.0 + jnp.exp(-gate_pre)) * up_pre).astype(jnp.bfloat16)
    hidden = hidden_ref[...]
    for start in range(0, width, tile):
        cols = slice(start, start + tile)
        o = (dot(hidden, dn_ref[0, :, cols]) * scale).astype(jnp.bfloat16)
        o_ref[:, own, cols] = o.reshape(group_count, capacity, tile)

    @pl.when(step == local_count - 1)
    def _():
        def store(group, value):
            out_ref[group] = value

        combine(gates_ref[...], o_ref, capacity, local_count, store)


def forward_rows(tokens, gates, weight_gu, weight_dn, capacity):
    group_count, token_count, width = tokens.shape
    local_count, hidden_units = weight_dn.shape[:2]
    whole = lambda shape: pl.BlockSpec(shape, lambda e: (0,) * len(shape))
    placed = (group_count, local_count * capacity, width)
    return pl.pallas_call(
        functools.partial(forward_kernel, capacity),
        grid=(local_count,),
        in_specs=[
            whole((group_count, token_count, width)),
            whole((group_count * local_count, token_count)),
            pl.BlockSpec((1, width, 2 * hidden_units), lambda e: (e, 0, 0)),
            pl.BlockSpec((1, hidden_units, width), lambda e: (e, 0, 0)),
        ],
        out_specs=whole((group_count, token_count, width)),
        out_shape=jax.ShapeDtypeStruct((group_count, token_count, width), jnp.bfloat16),
        scratch_shapes=[
            pltpu.VMEM(placed, jnp.bfloat16),
            pltpu.VMEM(placed[:2] + (128,), jnp.float32),
            pltpu.VMEM((group_count * capacity, hidden_units), jnp.bfloat16),
            pltpu.VMEM(placed, jnp.bfloat16),
        ],
        compiler_params=params(),
        cost_estimate=light(),
        name="forward_rows",
    )(tokens, gates.reshape(-1, token_count), weight_gu, weight_dn)


def gradient_kernel(
    which_ref, h_ref, c_ref, hidden_ref, d_ref, far_1_ref, far_2_ref, far_3_ref, gu_ref, dn_ref,
    out_gu_ref, out_dn_ref, far_c_ref, far_h_ref, far_hidden_ref, far_d_ref,
):
    step = pl.program_id(0)
    row_count = far_c_ref.shape[0]

    @pl.when(step == 0)
    def _():
        for target, base in ((far_c_ref, 0), (far_h_ref, row_count)):
            for send, there, part in overlaps(row_count, base, base + row_count):
                target[part] = (far_1_ref, far_2_ref, far_3_ref)[send][there]
        hidden_gradients(
            far_h_ref[...], far_c_ref[...], gu_ref, dn_ref, far_hidden_ref, far_d_ref
        )

    def columns(size):
        return pl.ds(pl.multiple_of(step * size, size), size)

    first = ((0,), (0,))
    cols = columns(out_gu_ref.shape[0])
    out_gu_ref[...] = (
        dot(h_ref[0, :, cols], d_ref[...], first)
        + dot(far_h_ref[:, cols], far_d_ref[...], first)
    ).astype(jnp.bfloat16)
    cols = columns(out_dn_ref.shape[0])
    out_dn_ref[...] = (
        dot(hidden_ref[:, cols], c_ref[0], first)
        + dot(far_hidden_ref[:, cols], far_c_ref[...], first)
    ).astype(jnp.bfloat16)


def weight_gradients(which, rows_h, rows_c, hidden, d, far, weight_gu, weight_dn):
    _, row_count, width = rows_h.shape
    hidden_units = weight_dn.shape[1]
    steps = width // tile
    whole = lambda shape: pl.BlockSpec(shape, lambda i, which: (0,) * len(shape))
    kept = lambda shape: pl.BlockSpec((1,) + shape, lambda i, which: (which[1], 0, 0))
    rows_spec = pl.BlockSpec((1, row_count, width), lambda i, which: (1, 0, 0))
    return pl.pallas_call(
        gradient_kernel,
        grid_spec=pltpu.PrefetchScalarGridSpec(
            num_scalar_prefetch=1,
            grid=(steps,),
            in_specs=[
                rows_spec,
                rows_spec,
                whole((row_count, hidden_units)),
                whole((row_count, 2 * hidden_units)),
                *[whole(part.shape) for part in far],
                kept((width, 2 * hidden_units)),
                kept((hidden_units, width)),
            ],
            out_specs=[
                pl.BlockSpec((width // steps, 2 * hidden_units), lambda i, which: (i, 0)),
                pl.BlockSpec((hidden_units // steps, width), lambda i, which: (i, 0)),
            ],
            scratch_shapes=[
                pltpu.VMEM((row_count, width), jnp.bfloat16),
                pltpu.VMEM((row_count, width), jnp.bfloat16),
                pltpu.VMEM((row_count, hidden_units), jnp.bfloat16),
                pltpu.VMEM((row_count, 2 * hidden_units), jnp.bfloat16),
            ],
        ),
        out_shape=[
            jax.ShapeDtypeStruct((width, 2 * hidden_units), jnp.bfloat16),
            jax.ShapeDtypeStruct((hidden_units, width), jnp.bfloat16),
        ],
        compiler_params=params(),
        cost_estimate=light(),
        name="weight_gradients",
    )(which, rows_h, rows_c, hidden, d, *far, weight_gu, weight_dn)


def swap_cores(value):
    return lax.ppermute(value, "expert", [(i, i ^ 1) for i in range(lax.axis_size("expert"))])


def exchange_sums(chip):
    group_count = lax.axis_size("expert")
    lines = [list(range(c, group_count, 2)) for c in range(2)]
    return lax.all_to_all(
        chip, "expert", split_axis=0, concat_axis=0, tiled=True, axis_index_groups=lines
    )


def per_device(
    x_fwd, gate_fwd, route_fwd, x_bwd, gate_bwd, route_bwd, cotangent, norm_gain, w_gate_up, w_down
):
    group_count = lax.axis_size("expert")
    section_count = lax.axis_size("pipe")
    local_count = w_gate_up.shape[1]
    expert_count = local_count * group_count
    token_count, model_width = x_fwd.shape
    pick_count = route_fwd.shape[1]
    capacity = token_count * pick_count * 4 // (3 * expert_count)
    weight_gu = w_gate_up[0]
    weight_dn = w_down[0]

    upper_half = (lax.axis_index("pipe") >= section_count // 2).astype(jnp.int32)
    which = jnp.stack([1 - upper_half, upper_half])
    core = lax.axis_index("expert") % 2
    chips = 2 * jnp.arange(group_count // 2, dtype=jnp.int32)
    order = jnp.concatenate([chips + core, chips + 1 - core])
    sides = jnp.stack([core, 1 - core])

    bwd_hat, bwd_scale = normalize(x_bwd)
    bwd_normed = (bwd_hat * norm_gain).astype(jnp.bfloat16)
    fwd_normed = (normalize(x_fwd)[0] * norm_gain).astype(jnp.bfloat16)
    send_gates = jnp.stack(
        [
            expert_gates(gate_fwd, route_fwd, expert_count),
            expert_gates(gate_bwd, route_bwd, expert_count),
        ]
    ).reshape(2, group_count, local_count, token_count)
    recv_gates = lax.all_to_all(
        send_gates.transpose(1, 0, 2, 3), "expert", split_axis=0, concat_axis=0, tiled=True
    )
    gates_f = recv_gates[:, 0]
    gates_b = recv_gates[:, 1][order][:, which]
    gathered_bwd = lax.all_gather(
        jnp.stack([cotangent, bwd_normed])[None], "expert", axis=0, tiled=True
    )
    gathered_fwd = lax.all_gather(fwd_normed[None], "expert", axis=0, tiled=True)

    mirror = [(i, section_count - 1 - i) for i in range(section_count)]
    rows_c, rows_h, *give = place_rows(gathered_bwd, gates_b, sides, capacity)
    far = [lax.ppermute(part, "pipe", mirror) for part in give]

    own_dh, other_dh, keep_hidden, keep_d = backward_rows(
        rows_h, rows_c, weight_gu, weight_dn, gates_b, which, capacity
    )
    other_dh, far[0] = lax.optimization_barrier((other_dh, far[0]))
    other_dh = swap_cores(other_dh)
    middle = token_count // 2
    chip_dh = [
        (own_dh[:, part].astype(jnp.float32) + other_dh[:, part].astype(jnp.float32)).astype(
            jnp.bfloat16
        )
        for part in (slice(0, middle), slice(middle, token_count))
    ]
    chip_dh, gathered_fwd = lax.optimization_barrier((chip_dh, gathered_fwd))
    parts_dh = [exchange_sums(chip) for chip in chip_dh]

    partial_y = forward_rows(gathered_fwd, gates_f, weight_gu, weight_dn, capacity)
    partial_y, parts_dh[0], far[1] = lax.optimization_barrier((partial_y, parts_dh[0], far[1]))
    y_fwd = lax.psum_scatter(
        partial_y.reshape(group_count * token_count, model_width),
        "expert",
        scatter_dimension=0,
        tiled=True,
    )

    out_gu, out_dn = weight_gradients(
        which, rows_h, rows_c, keep_hidden, keep_d, far, weight_gu, weight_dn
    )

    dh_sum = jnp.concatenate([jnp.sum(part.astype(jnp.float32), axis=0) for part in parts_dh])
    scaled_dh = norm_gain * dh_sum
    dx_bwd = (
        bwd_scale * (scaled_dh - bwd_hat * jnp.mean(bwd_hat * scaled_dh, axis=-1, keepdims=True))
    ).astype(jnp.bfloat16)
    return (y_fwd, dx_bwd, out_gu[None, None], out_dn[None, None])


def solution(mesh):
    rows = P(("pipe", "expert"), None)
    experts = P("pipe", "expert", None, None)
    return jax.shard_map(
        per_device,
        mesh=mesh,
        in_specs=(rows,) * 7 + (P(), experts, experts),
        out_specs=(rows, rows, experts, experts),
        check_vma=False,
    )
```

```python
import functools

import jax
import jax.numpy as jnp
from jax import lax
from jax.experimental import pallas as pl
from jax.experimental.pallas import tpu as pltpu
from jax.sharding import PartitionSpec as P

norm_eps = 1e-06
tile = 256
vmem_bytes = 56 * 1024 * 1024


def params():
    return pltpu.CompilerParams(
        dimension_semantics=("arbitrary",), vmem_limit_bytes=vmem_bytes
    )


def light():
    return pl.CostEstimate(flops=1000, bytes_accessed=1000, transcendentals=0)


def dot(a, b, contract=((1,), (0,))):
    return lax.dot_general(a, b, (contract, ((), ())), preferred_element_type=jnp.float32)


def normalize(inputs):
    values = inputs.astype(jnp.float32)
    scale = lax.rsqrt(jnp.mean(values * values, axis=-1, keepdims=True) + norm_eps)
    return (values * scale, scale)


def norm_kernel(x_ref, gain_ref, *refs):
    out_ref = refs[-1]
    values = x_ref[...].astype(jnp.float32)
    scale = lax.rsqrt(jnp.mean(values * values, axis=-1, keepdims=True) + norm_eps)
    out_ref[len(refs) - 1] = (values * scale * gain_ref[...][None, :]).astype(jnp.bfloat16)
    for index, other_ref in enumerate(refs[:-1]):
        out_ref[index] = other_ref[...]


def normed(x, gain, *others):
    return pl.pallas_call(
        norm_kernel,
        out_shape=jax.ShapeDtypeStruct((1 + len(others),) + x.shape, jnp.bfloat16),
        cost_estimate=light(),
        name="normed",
    )(x, gain, *others)


def expert_gates(gates, routes, expert_count):
    chosen = routes[None, :, :] == jnp.arange(expert_count, dtype=jnp.int32)[:, None, None]
    return jnp.sum(jnp.where(chosen, gates[None], 0.0), axis=-1)


def ranks(gates):
    named = gates > 0.0
    token_count = gates.shape[1]
    upto = lax.broadcasted_iota(jnp.int32, (token_count, token_count), 0) <= (
        lax.broadcasted_iota(jnp.int32, (token_count, token_count), 1)
    )
    count = dot(
        jnp.where(named, 1.0, 0.0).astype(jnp.bfloat16), jnp.where(upto, 1.0, 0.0).astype(jnp.bfloat16)
    )
    return jnp.where(named, count - 1.0, -1.0)


def onehot_rows(rank, group, local_count, capacity):
    token_count = rank.shape[1]
    slots = lax.broadcasted_iota(jnp.int32, (capacity, token_count), 0).astype(jnp.float32)
    parts = []
    for local in range(local_count):
        row = group * local_count + local
        parts.append(jnp.where(rank[row : row + 1, :] == slots, 1.0, 0.0))
    return jnp.concatenate(parts, axis=0)


def slot_gates(onehot, gates, group, local_count, capacity):
    parts = []
    for local in range(local_count):
        row = group * local_count + local
        own = onehot[local * capacity : (local + 1) * capacity]
        parts.append(jnp.sum(own * gates[row : row + 1, :], axis=1, keepdims=True))
    return jnp.concatenate(parts, axis=0)


def cuts(row_count):
    ends = [0, row_count * 5 // 8, row_count * 35 // 32, row_count * 2]
    return [(start, end) for start, end in zip(ends[:-1], ends[1:])]


def overlaps(row_count, start, end):
    for send, (low, high) in enumerate(cuts(row_count)):
        first, last = max(start, low), min(end, high)
        if first < last:
            yield send, slice(first - low, last - low), slice(first - start, last - start)


def place_kernel(
    capacity, sides_ref, c_ref, h_ref, gates_ref, keep_c_ref, keep_h_ref, *give_refs
):
    half = h_ref.shape[0]
    row_count = 2 * half * capacity

    def place(side):
        gates = gates_ref[0]
        rank = ranks(gates)
        for group in range(half):
            onehot = onehot_rows(rank, group, 2, capacity)
            scale = slot_gates(onehot, gates, group, 2, capacity)
            onehot = onehot.astype(jnp.bfloat16)
            rows_c = (dot(onehot, c_ref[group, 0, 0]) * scale).astype(jnp.bfloat16)
            rows_h = dot(onehot, h_ref[group, 0, 0]).astype(jnp.bfloat16)
            here = slice(group * capacity, (group + 1) * capacity)
            keep_c_ref[here] = rows_c[:capacity]
            keep_h_ref[here] = rows_h[:capacity]
            first = (side * half + group) * capacity
            for base, rows in ((first, rows_c), (row_count + first, rows_h)):
                for send, there, part in overlaps(row_count, base, base + capacity):
                    give_refs[send][there] = rows[capacity:][part]

    for side in range(2):
        pl.when(pl.program_id(0) == side)(functools.partial(place, side))


def place_rows(tokens, gates, sides, capacity):
    group_count, _, token_count, width = tokens.shape
    half = group_count // 2
    row_count = group_count * capacity
    rows_spec = pl.BlockSpec((row_count // 2, width), lambda i, sides: (i, 0))
    give_shapes = [(end - start, width) for start, end in cuts(row_count)]
    block = (half, 1, 1, token_count, width)
    tokens = tokens.reshape(half, 2, 2, token_count, width)
    return pl.pallas_call(
        functools.partial(place_kernel, capacity),
        grid_spec=pltpu.PrefetchScalarGridSpec(
            num_scalar_prefetch=1,
            grid=(2,),
            in_specs=[
                pl.BlockSpec(block, lambda i, sides: (0, sides[i], 0, 0, 0)),
                pl.BlockSpec(block, lambda i, sides: (0, sides[i], 1, 0, 0)),
                pl.BlockSpec((1, half * 2, token_count), lambda i, sides: (i, 0, 0)),
            ],
            out_specs=[rows_spec, rows_spec]
            + [pl.BlockSpec(shape, lambda i, sides: (0, 0)) for shape in give_shapes],
        ),
        out_shape=[jax.ShapeDtypeStruct((row_count, width), jnp.bfloat16)] * 2
        + [jax.ShapeDtypeStruct(shape, jnp.bfloat16) for shape in give_shapes],
        compiler_params=params(),
        cost_estimate=light(),
        name="place_rows",
    )(sides, tokens, tokens, gates.reshape(2, half * 2, token_count))


class Copies:
    def __init__(self, sems):
        self.sems = sems
        self.count = 0
        self.waiting = {}

    def start(self, name, source, target):
        copy = pltpu.make_async_copy(source, target, self.sems.at[self.count])
        self.count += 1
        copy.start()
        self.waiting.setdefault(name, []).append(copy)

    def wait(self, name):
        for copy in self.waiting.pop(name, []):
            copy.wait()

    def wait_all(self):
        for name in list(self.waiting):
            self.wait(name)


def weight_copies(copies, expert, source, gu_ref, dn_ref, gu, dn):
    hidden_units = dn.shape[1]
    for start in range(0, hidden_units, tile):
        for base in (0, hidden_units):
            cols = slice(base + start, base + start + tile)
            copies.start(("gu", expert, start), gu_ref.at[source, :, cols], gu.at[expert, :, cols])
        rows = slice(start, start + tile)
        copies.start(("dn", expert, start), dn_ref.at[source, rows], dn.at[expert, rows])


def hidden_gradients(copies, expert, h, c, gu, dn, hidden_ref, d_ref):
    hidden_units = dn.shape[1]
    for start in range(0, hidden_units, tile):
        cols = slice(start, start + tile)
        up_cols = slice(hidden_units + start, hidden_units + start + tile)
        copies.wait(("gu", expert, start))
        gate_pre = dot(h(), gu[expert, :, cols])
        up_pre = dot(h(), gu[expert, :, up_cols])
        copies.wait(("dn", expert, start))
        back = dot(c(), dn[expert, cols, :], ((1,), (1,)))
        squash = 1.0 / (1.0 + jnp.exp(-gate_pre))
        activated = gate_pre * squash
        if hidden_ref is not None:
            hidden_ref[:, cols] = (activated * up_pre).astype(jnp.bfloat16)
        d_ref[:, cols] = (back * up_pre * squash * (1.0 + gate_pre * (1.0 - squash))).astype(
            jnp.bfloat16
        )
        d_ref[:, up_cols] = (back * activated).astype(jnp.bfloat16)


anywhere = pl.BlockSpec(memory_space=pl.ANY)
vector = pl.BlockSpec(memory_space=pltpu.VMEM)
scalar = pl.BlockSpec(memory_space=pltpu.SMEM)


def kernel_params():
    return pltpu.CompilerParams(vmem_limit_bytes=vmem_bytes)


def combine(gates, rows_ref, capacity, store):
    rank = ranks(gates)
    for group in range(rows_ref.shape[0]):
        onehot = onehot_rows(rank, group, 2, capacity).T.astype(jnp.bfloat16)
        store(group, dot(onehot, rows_ref[group]).astype(jnp.bfloat16))


def backward_kernel(
    capacity, which_ref, gates_ref, keep_c_ref, keep_h_ref, give_1_ref, give_2_ref, give_3_ref,
    gu_ref, dn_ref, own_ref, other_ref, hidden_out, d_out,
    c, h, gu, dn, hidden, d, dh, sums, sems,
):
    row_count, width = keep_c_ref.shape
    group_count = row_count // capacity
    half = group_count // 2
    copies = Copies(sems)
    copies.start("h0", keep_h_ref, h.at[0])
    copies.start("c0", keep_c_ref, c.at[0])
    weight_copies(copies, 0, which_ref[0], gu_ref, dn_ref, gu, dn)
    for name, target, base in (("c1", c, 0), ("h1", h, row_count)):
        for send, there, part in overlaps(row_count, base, base + row_count):
            copies.start(
                name, (give_1_ref, give_2_ref, give_3_ref)[send].at[there], target.at[1, part]
            )
    weight_copies(copies, 1, which_ref[1], gu_ref, dn_ref, gu, dn)
    for expert in range(2):
        copies.wait("h%d" % expert)
        copies.wait("c%d" % expert)
        hidden_gradients(
            copies,
            expert,
            lambda: h[expert],
            lambda: c[expert],
            gu,
            dn,
            hidden if expert == 0 else None,
            d.at[expert],
        )
        if expert == 0:
            copies.start("out", hidden, hidden_out)
            copies.start("out", d.at[0], d_out)
        for start in range(0, width, tile):
            cols = slice(start, start + tile)
            part = dot(d[expert], gu[expert, cols, :], ((1,), (1,))).astype(jnp.bfloat16)
            dh[:, expert * capacity : (expert + 1) * capacity, cols] = part.reshape(
                group_count, capacity, tile
            )

    def store(group, value):
        sums[group] = value
        target = own_ref if group < half else other_ref
        copies.start("out", sums.at[group], target.at[group % half])

    combine(gates_ref[...], dh, capacity, store)
    copies.wait_all()


def backward_rows(keep_c, keep_h, give, weight_gu, weight_dn, gates, which, capacity):
    row_count, width = keep_c.shape
    hidden_units = weight_dn.shape[1]
    group_count = row_count // capacity
    token_count = gates.shape[-1]
    half = (group_count // 2, token_count, width)
    tiles = hidden_units // tile
    bf16 = jnp.bfloat16
    return pl.pallas_call(
        functools.partial(backward_kernel, capacity),
        in_specs=[scalar, vector] + [anywhere] * 7,
        out_specs=[anywhere] * 4,
        out_shape=[
            jax.ShapeDtypeStruct(half, bf16),
            jax.ShapeDtypeStruct(half, bf16),
            jax.ShapeDtypeStruct((row_count, hidden_units), bf16),
            jax.ShapeDtypeStruct((row_count, 2 * hidden_units), bf16),
        ],
        scratch_shapes=[
            pltpu.VMEM((2, row_count, width), bf16),
            pltpu.VMEM((2, row_count, width), bf16),
            pltpu.VMEM(weight_gu.shape, bf16),
            pltpu.VMEM(weight_dn.shape, bf16),
            pltpu.VMEM((row_count, hidden_units), bf16),
            pltpu.VMEM((2, row_count, 2 * hidden_units), bf16),
            pltpu.VMEM((group_count, 2 * capacity, width), bf16),
            pltpu.VMEM((group_count, token_count, width), bf16),
            pltpu.SemaphoreType.DMA((8 + 6 * tiles + group_count,)),
        ],
        compiler_params=kernel_params(),
        cost_estimate=light(),
        name="backward_rows",
    )(which, gates.reshape(-1, token_count), keep_c, keep_h, *give, weight_gu, weight_dn)


def forward_kernel(
    capacity, gates_ref, tokens_ref, gu_ref, dn_ref, out_ref,
    tokens, gu, dn, rows, scales, hidden, o, sums, sems,
):
    group_count, _, width = tokens.shape
    hidden_units = dn.shape[1]
    row_count = group_count * capacity
    copies = Copies(sems)
    for group in range(group_count):
        copies.start(("tokens", group), tokens_ref.at[group], tokens.at[group])
    for expert in range(2):
        weight_copies(copies, expert, expert, gu_ref, dn_ref, gu, dn)
    gates = gates_ref[...]
    rank = ranks(gates)
    for group in range(group_count):
        onehot = onehot_rows(rank, group, 2, capacity)
        scale = slot_gates(onehot, gates, group, 2, capacity)
        copies.wait(("tokens", group))
        placed = dot(onehot.astype(jnp.bfloat16), tokens[group]).astype(jnp.bfloat16)
        here = slice(group * capacity, (group + 1) * capacity)
        for expert in range(2):
            own = slice(expert * capacity, (expert + 1) * capacity)
            rows[expert, here] = placed[own]
            scales[expert, here] = jnp.broadcast_to(scale[own], (capacity, 128))
    for expert in range(2):
        for start in range(0, hidden_units, tile):
            cols = slice(start, start + tile)
            up_cols = slice(hidden_units + start, hidden_units + start + tile)
            copies.wait(("gu", expert, start))
            gate_pre = dot(rows[expert], gu[expert, :, cols])
            up_pre = dot(rows[expert], gu[expert, :, up_cols])
            hidden[:, cols] = (gate_pre / (1.0 + jnp.exp(-gate_pre)) * up_pre).astype(jnp.bfloat16)
        for start in range(0, hidden_units, tile):
            copies.wait(("dn", expert, start))
        scale = scales[expert][:, :1]
        for start in range(0, width, tile):
            cols = slice(start, start + tile)
            part = (dot(hidden[...], dn[expert, :, cols]) * scale).astype(jnp.bfloat16)
            o[:, expert * capacity : (expert + 1) * capacity, cols] = part.reshape(
                group_count, capacity, tile
            )

    def store(group, value):
        sums[group] = value
        copies.start("out", sums.at[group], out_ref.at[group])

    combine(gates, o, capacity, store)
    copies.wait_all()


def forward_rows(tokens, gates, weight_gu, weight_dn, capacity):
    group_count, token_count, width = tokens.shape
    hidden_units = weight_dn.shape[1]
    row_count = group_count * capacity
    tiles = hidden_units // tile
    bf16 = jnp.bfloat16
    return pl.pallas_call(
        functools.partial(forward_kernel, capacity),
        in_specs=[vector] + [anywhere] * 3,
        out_specs=anywhere,
        out_shape=jax.ShapeDtypeStruct((group_count, token_count, width), bf16),
        scratch_shapes=[
            pltpu.VMEM((group_count, token_count, width), bf16),
            pltpu.VMEM(weight_gu.shape, bf16),
            pltpu.VMEM(weight_dn.shape, bf16),
            pltpu.VMEM((2, row_count, width), bf16),
            pltpu.VMEM((2, row_count, 128), jnp.float32),
            pltpu.VMEM((row_count, hidden_units), bf16),
            pltpu.VMEM((group_count, 2 * capacity, width), bf16),
            pltpu.VMEM((group_count, token_count, width), bf16),
            pltpu.SemaphoreType.DMA((6 * tiles + 2 * group_count,)),
        ],
        compiler_params=kernel_params(),
        cost_estimate=light(),
        name="forward_rows",
    )(gates.reshape(-1, token_count), tokens, weight_gu, weight_dn)


def gradient_kernel(
    which_ref, keep_c_ref, keep_h_ref, hidden_ref, d_ref, far_1_ref, far_2_ref, far_3_ref,
    gu_ref, dn_ref, gu_out, dn_out, c, h, hidden, d, gu, dn, gu_sums, dn_sums, sems,
):
    row_count, width = keep_c_ref.shape
    hidden_units = dn.shape[1]
    far = slice(row_count, 2 * row_count)
    near = slice(0, row_count)
    copies = Copies(sems)
    for name, target, base in (("far", h, row_count), ("far", c, 0)):
        for send, there, part in overlaps(row_count, base, base + row_count):
            place = slice(row_count + part.start, row_count + part.stop)
            copies.start(
                name, (far_1_ref, far_2_ref, far_3_ref)[send].at[there], target.at[place]
            )
    weight_copies(copies, 0, which_ref[0], gu_ref, dn_ref, gu, dn)
    copies.start("hidden", hidden_ref, hidden.at[near])
    copies.start("c", keep_c_ref, c.at[near])
    copies.start("d", d_ref, d.at[near])
    copies.start("h", keep_h_ref, h.at[near])
    copies.wait("far")
    hidden_gradients(
        copies, 0, lambda: h[far], lambda: c[far], gu, dn, hidden.at[far], d.at[far]
    )
    first = ((0,), (0,))
    copies.wait("hidden")
    copies.wait("c")
    for start in range(0, hidden_units, tile):
        cols = slice(start, start + tile)
        dn_sums[cols] = dot(hidden[:, cols], c[...], first).astype(jnp.bfloat16)
        copies.start("out", dn_sums.at[cols], dn_out.at[cols])
    copies.wait("d")
    copies.wait("h")
    for start in range(0, width, tile):
        cols = slice(start, start + tile)
        gu_sums[cols] = dot(h[:, cols], d[...], first).astype(jnp.bfloat16)
        copies.start("out", gu_sums.at[cols], gu_out.at[cols])
    copies.wait_all()


def weight_gradients(which, keep_c, keep_h, hidden, d, far, weight_gu, weight_dn):
    row_count, width = keep_c.shape
    hidden_units = weight_dn.shape[1]
    bf16 = jnp.bfloat16
    gu_shape = (width, 2 * hidden_units)
    dn_shape = (hidden_units, width)
    count = 4 + 4 + 4 * (hidden_units // tile) + width // tile
    return pl.pallas_call(
        gradient_kernel,
        in_specs=[scalar] + [anywhere] * 9,
        out_specs=[anywhere] * 2,
        out_shape=[jax.ShapeDtypeStruct(gu_shape, bf16), jax.ShapeDtypeStruct(dn_shape, bf16)],
        scratch_shapes=[
            pltpu.VMEM((2 * row_count, width), bf16),
            pltpu.VMEM((2 * row_count, width), bf16),
            pltpu.VMEM((2 * row_count, hidden_units), bf16),
            pltpu.VMEM((2 * row_count, 2 * hidden_units), bf16),
            pltpu.VMEM((1,) + gu_shape, bf16),
            pltpu.VMEM((1,) + dn_shape, bf16),
            pltpu.VMEM(gu_shape, bf16),
            pltpu.VMEM(dn_shape, bf16),
            pltpu.SemaphoreType.DMA((count,)),
        ],
        compiler_params=kernel_params(),
        cost_estimate=light(),
        name="weight_gradients",
    )(which, keep_c, keep_h, hidden, d, *far, weight_gu, weight_dn)


def swap_cores(value):
    return lax.ppermute(value, "expert", [(i, i ^ 1) for i in range(lax.axis_size("expert"))])


def exchange_sums(chip):
    group_count = lax.axis_size("expert")
    lines = [list(range(c, group_count, 2)) for c in range(2)]
    return lax.all_to_all(
        chip, "expert", split_axis=0, concat_axis=0, tiled=True, axis_index_groups=lines
    )


def per_device(
    x_fwd, gate_fwd, route_fwd, x_bwd, gate_bwd, route_bwd, cotangent, norm_gain, w_gate_up, w_down
):
    group_count = lax.axis_size("expert")
    section_count = lax.axis_size("pipe")
    local_count = w_gate_up.shape[1]
    expert_count = local_count * group_count
    token_count, model_width = x_fwd.shape
    pick_count = route_fwd.shape[1]
    capacity = token_count * pick_count * 4 // (3 * expert_count)
    weight_gu = w_gate_up[0]
    weight_dn = w_down[0]

    upper_half = (lax.axis_index("pipe") >= section_count // 2).astype(jnp.int32)
    which = jnp.stack([upper_half, 1 - upper_half])
    core = lax.axis_index("expert") % 2
    chips = 2 * jnp.arange(group_count // 2, dtype=jnp.int32)
    order = jnp.concatenate([chips + core, chips + 1 - core])
    sides = jnp.stack([core, 1 - core])

    send_gates = jnp.stack(
        [
            expert_gates(gate_fwd, route_fwd, expert_count),
            expert_gates(gate_bwd, route_bwd, expert_count),
        ]
    ).reshape(2, group_count, local_count, token_count)
    recv_gates = lax.all_to_all(
        send_gates.transpose(1, 0, 2, 3), "expert", split_axis=0, concat_axis=0, tiled=True
    )
    gates_f = recv_gates[:, 0]
    gates_b = recv_gates[:, 1][order][:, which]
    gathered_bwd = lax.all_gather(
        normed(x_bwd, norm_gain, cotangent)[None], "expert", axis=0, tiled=True
    )
    gathered_fwd = lax.all_gather(normed(x_fwd, norm_gain), "expert", axis=0, tiled=True)

    mirror = [(i, section_count - 1 - i) for i in range(section_count)]
    keep_c, keep_h, *give = place_rows(gathered_bwd, gates_b, sides, capacity)
    far = [lax.ppermute(part, "pipe", mirror) for part in give]

    own_dh, other_dh, keep_hidden, keep_d = backward_rows(
        keep_c, keep_h, give, weight_gu, weight_dn, gates_b, which, capacity
    )
    other_dh, far[0] = lax.optimization_barrier((other_dh, far[0]))
    other_dh = swap_cores(other_dh)
    middle = token_count // 2
    chip_dh = [
        (own_dh[:, part].astype(jnp.float32) + other_dh[:, part].astype(jnp.float32)).astype(
            jnp.bfloat16
        )
        for part in (slice(0, middle), slice(middle, token_count))
    ]
    chip_dh, gathered_fwd = lax.optimization_barrier((chip_dh, gathered_fwd))
    parts_dh = [exchange_sums(chip) for chip in chip_dh]

    partial_y = forward_rows(gathered_fwd, gates_f, weight_gu, weight_dn, capacity)
    partial_y, parts_dh[0], far[1] = lax.optimization_barrier((partial_y, parts_dh[0], far[1]))
    y_fwd = lax.psum_scatter(
        partial_y.reshape(group_count * token_count, model_width),
        "expert",
        scatter_dimension=0,
        tiled=True,
    )

    out_gu, out_dn = weight_gradients(
        which, keep_c, keep_h, keep_hidden, keep_d, far, weight_gu, weight_dn
    )

    dh_sum = jnp.concatenate([jnp.sum(part.astype(jnp.float32), axis=0) for part in parts_dh])
    bwd_hat, bwd_scale = normalize(x_bwd)
    scaled_dh = norm_gain * dh_sum
    dx_bwd = (
        bwd_scale * (scaled_dh - bwd_hat * jnp.mean(bwd_hat * scaled_dh, axis=-1, keepdims=True))
    ).astype(jnp.bfloat16)
    return (y_fwd, dx_bwd, out_gu[None, None], out_dn[None, None])


def solution(mesh):
    rows = P(("pipe", "expert"), None)
    experts = P("pipe", "expert", None, None)
    return jax.shard_map(
        per_device,
        mesh=mesh,
        in_specs=(rows,) * 7 + (P(), experts, experts),
        out_specs=(rows, rows, experts, experts),
        check_vma=False,
    )
```

```python
import functools

import jax
import jax.numpy as jnp
from jax import lax
from jax.experimental import pallas as pl
from jax.experimental.pallas import tpu as pltpu
from jax.sharding import PartitionSpec as P

norm_eps = 1e-06
tile = 256
vmem_bytes = 56 * 1024 * 1024
shared_vmem_bytes = 28 * 1024 * 1024


def params():
    return pltpu.CompilerParams(
        dimension_semantics=("arbitrary",), vmem_limit_bytes=shared_vmem_bytes
    )


def light():
    return pl.CostEstimate(flops=1000, bytes_accessed=1000, transcendentals=0)


def dot(a, b, contract=((1,), (0,))):
    return lax.dot_general(a, b, (contract, ((), ())), preferred_element_type=jnp.float32)


def normalize(inputs):
    values = inputs.astype(jnp.float32)
    scale = lax.rsqrt(jnp.mean(values * values, axis=-1, keepdims=True) + norm_eps)
    return (values * scale, scale)


def norm_kernel(x_ref, gain_ref, *refs):
    out_ref = refs[-1]
    values = x_ref[...].astype(jnp.float32)
    scale = lax.rsqrt(jnp.mean(values * values, axis=-1, keepdims=True) + norm_eps)
    out_ref[len(refs) - 1] = (values * scale * gain_ref[...][None, :]).astype(jnp.bfloat16)
    for index, other_ref in enumerate(refs[:-1]):
        out_ref[index] = other_ref[...]


def normed(x, gain, *others):
    return pl.pallas_call(
        norm_kernel,
        out_shape=jax.ShapeDtypeStruct((1 + len(others),) + x.shape, jnp.bfloat16),
        cost_estimate=light(),
        name="normed",
    )(x, gain, *others)


def expert_gates(gates, routes, expert_count):
    chosen = routes[None, :, :] == jnp.arange(expert_count, dtype=jnp.int32)[:, None, None]
    return jnp.sum(jnp.where(chosen, gates[None], 0.0), axis=-1)


def ranks(gates):
    named = gates > 0.0
    token_count = gates.shape[1]
    upto = lax.broadcasted_iota(jnp.int32, (token_count, token_count), 0) <= (
        lax.broadcasted_iota(jnp.int32, (token_count, token_count), 1)
    )
    count = dot(
        jnp.where(named, 1.0, 0.0).astype(jnp.bfloat16), jnp.where(upto, 1.0, 0.0).astype(jnp.bfloat16)
    )
    return jnp.where(named, count - 1.0, -1.0)


def onehot_rows(rank, group, local_count, capacity):
    token_count = rank.shape[1]
    slots = lax.broadcasted_iota(jnp.int32, (capacity, token_count), 0).astype(jnp.float32)
    parts = []
    for local in range(local_count):
        row = group * local_count + local
        parts.append(jnp.where(rank[row : row + 1, :] == slots, 1.0, 0.0))
    return jnp.concatenate(parts, axis=0)


def slot_gates(onehot, gates, group, local_count, capacity):
    parts = []
    for local in range(local_count):
        row = group * local_count + local
        own = onehot[local * capacity : (local + 1) * capacity]
        parts.append(jnp.sum(own * gates[row : row + 1, :], axis=1, keepdims=True))
    return jnp.concatenate(parts, axis=0)


def cuts(row_count):
    ends = [0, row_count * 9 // 32, row_count // 2, row_count]
    return [(start, end) for start, end in zip(ends[:-1], ends[1:])]


def overlaps(row_count, start, end):
    for send, (low, high) in enumerate(cuts(row_count)):
        first, last = max(start, low), min(end, high)
        if first < last:
            yield send, slice(first - low, last - low), slice(first - start, last - start)


def place_kernel(
    capacity, sides_ref, c_ref, h_ref, gates_ref, keep_c_ref, keep_h_ref, *give_refs
):
    half = h_ref.shape[0]
    row_count = 2 * half * capacity

    def place(side):
        gates = gates_ref[0]
        rank = ranks(gates)
        for group in range(half):
            onehot = onehot_rows(rank, group, 2, capacity)
            scale = slot_gates(onehot, gates, group, 2, capacity)
            onehot = onehot.astype(jnp.bfloat16)
            rows_c = (dot(onehot, c_ref[group, 0, 0]) * scale).astype(jnp.bfloat16)
            rows_h = dot(onehot, h_ref[group, 0, 0]).astype(jnp.bfloat16)
            here = slice(group * capacity, (group + 1) * capacity)
            keep_c_ref[here] = rows_c[:capacity]
            keep_h_ref[here] = rows_h[:capacity]
            first = (side * half + group) * capacity
            for send, there, part in overlaps(row_count, first, first + capacity):
                give_refs[send][0, there] = rows_c[capacity:][part]
                give_refs[send][1, there] = rows_h[capacity:][part]

    for side in range(2):
        pl.when(pl.program_id(0) == side)(functools.partial(place, side))


def in_main(value):
    return pltpu.with_memory_space_constraint(value, pltpu.HBM)


def place_rows(tokens, gates, sides, capacity):
    group_count, _, token_count, width = tokens.shape
    half = group_count // 2
    row_count = group_count * capacity
    rows_spec = pl.BlockSpec((row_count // 2, width), lambda i, sides: (i, 0))
    give_shapes = [(2, end - start, width) for start, end in cuts(row_count)]
    block = (half, 1, 1, token_count, width)
    tokens = tokens.reshape(half, 2, 2, token_count, width)
    return pl.pallas_call(
        functools.partial(place_kernel, capacity),
        grid_spec=pltpu.PrefetchScalarGridSpec(
            num_scalar_prefetch=1,
            grid=(2,),
            in_specs=[
                pl.BlockSpec(block, lambda i, sides: (0, sides[i], 0, 0, 0)),
                pl.BlockSpec(block, lambda i, sides: (0, sides[i], 1, 0, 0)),
                pl.BlockSpec((1, half * 2, token_count), lambda i, sides: (i, 0, 0)),
            ],
            out_specs=[rows_spec, rows_spec]
            + [pl.BlockSpec(shape, lambda i, sides: (0, 0, 0)) for shape in give_shapes],
        ),
        out_shape=[pltpu.HBM((row_count, width), jnp.bfloat16)] * 2
        + [pltpu.HBM(shape, jnp.bfloat16) for shape in give_shapes],
        compiler_params=params(),
        cost_estimate=light(),
        name="place_rows",
    )(sides, in_main(tokens), in_main(tokens), gates.reshape(2, half * 2, token_count))


class Copies:
    def __init__(self, sems):
        self.sems = sems
        self.count = 0
        self.waiting = {}

    def start(self, name, source, target):
        copy = pltpu.make_async_copy(source, target, self.sems.at[self.count])
        self.count += 1
        copy.start()
        self.waiting.setdefault(name, []).append(copy)

    def wait(self, name):
        for copy in self.waiting.pop(name, []):
            copy.wait()

    def wait_all(self):
        for name in list(self.waiting):
            self.wait(name)


def weight_copies(copies, expert, source, gu_ref, dn_ref, gu, dn):
    hidden_units = dn.shape[1]
    for start in range(0, hidden_units, tile):
        for base in (0, hidden_units):
            cols = slice(base + start, base + start + tile)
            copies.start(("gu", expert, start), gu_ref.at[source, :, cols], gu.at[expert, :, cols])
        rows = slice(start, start + tile)
        copies.start(("dn", expert, start), dn_ref.at[source, rows], dn.at[expert, rows])


def down_copies(copies, expert, source, dn_ref, dn):
    for start in range(0, dn.shape[1], tile):
        part = slice(start, start + tile)
        copies.start(("dn", expert, start), dn_ref.at[source, part], dn.at[expert, part])


def hidden_gradients(copies, key, h, c, gu, dn, hidden_ref, d_ref):
    hidden_units = dn.shape[0]
    for start in range(0, hidden_units, tile):
        cols = slice(start, start + tile)
        up_cols = slice(hidden_units + start, hidden_units + start + tile)
        copies.wait(("gu", key, start))
        gate_pre = dot(h(), gu[:, cols])
        up_pre = dot(h(), gu[:, up_cols])
        copies.wait(("dn", key, start))
        back = dot(c(), dn[cols, :], ((1,), (1,)))
        squash = 1.0 / (1.0 + jnp.exp(-gate_pre))
        activated = gate_pre * squash
        if hidden_ref is not None:
            hidden_ref[:, cols] = (activated * up_pre).astype(jnp.bfloat16)
        d_ref[:, cols] = (back * up_pre * squash * (1.0 + gate_pre * (1.0 - squash))).astype(
            jnp.bfloat16
        )
        d_ref[:, up_cols] = (back * activated).astype(jnp.bfloat16)


anywhere = pl.BlockSpec(memory_space=pl.ANY)
vector = pl.BlockSpec(memory_space=pltpu.VMEM)
scalar = pl.BlockSpec(memory_space=pltpu.SMEM)


def in_vector(value):
    return pltpu.with_memory_space_constraint(value, pltpu.VMEM)


def kernel_params(limit=vmem_bytes):
    return pltpu.CompilerParams(vmem_limit_bytes=limit)


def combine(gates, rows_ref, capacity, store):
    rank = ranks(gates)
    for group in range(rows_ref.shape[0]):
        onehot = onehot_rows(rank, group, 2, capacity).T.astype(jnp.bfloat16)
        store(group, dot(onehot, rows_ref[group]).astype(jnp.bfloat16))


def backward_kernel(
    capacity, which_ref, gates_ref, keep_c_ref, keep_h_ref, give_1_ref, give_2_ref, give_3_ref,
    gu, dn_ref, own_ref, other_ref, hidden_out, d_out,
    c, h, dn, hidden, d, dh, sums, sems,
):
    row_count, width = keep_c_ref.shape
    group_count = row_count // capacity
    half = group_count // 2
    copies = Copies(sems)
    copies.start("h0", keep_h_ref, h.at[0])
    copies.start("c0", keep_c_ref, c.at[0])
    down_copies(copies, 0, which_ref[0], dn_ref, dn)
    for send, there, part in overlaps(row_count, 0, row_count):
        give_ref = (give_1_ref, give_2_ref, give_3_ref)[send]
        copies.start("c1", give_ref.at[0, there], c.at[1, part])
        copies.start("h1", give_ref.at[1, there], h.at[1, part])
    down_copies(copies, 1, which_ref[1], dn_ref, dn)
    for expert in range(2):
        source = which_ref[expert]
        copies.wait("h%d" % expert)
        copies.wait("c%d" % expert)
        hidden_gradients(
            copies,
            expert,
            lambda: h[expert],
            lambda: c[expert],
            gu.at[source],
            dn.at[expert],
            hidden if expert == 0 else None,
            d.at[expert],
        )
        if expert == 0:
            copies.start("out", hidden, hidden_out)
            copies.start("out", d.at[0], d_out)
        for start in range(0, width, tile):
            cols = slice(start, start + tile)
            part = dot(d[expert], gu[source, cols, :], ((1,), (1,))).astype(jnp.bfloat16)
            dh[:, expert * capacity : (expert + 1) * capacity, cols] = part.reshape(
                group_count, capacity, tile
            )

    def store(group, value):
        sums[group] = value
        target = own_ref if group < half else other_ref
        copies.start("out", sums.at[group], target.at[group % half])

    combine(gates_ref[...], dh, capacity, store)
    copies.wait_all()


def backward_rows(keep_c, keep_h, give, weight_gu, weight_dn, gates, which, capacity):
    row_count, width = keep_c.shape
    hidden_units = weight_dn.shape[1]
    group_count = row_count // capacity
    token_count = gates.shape[-1]
    half = (group_count // 2, token_count, width)
    bf16 = jnp.bfloat16
    return pl.pallas_call(
        functools.partial(backward_kernel, capacity),
        in_specs=[scalar, vector] + [anywhere] * 5 + [vector, anywhere],
        out_specs=[anywhere] * 4,
        out_shape=[
            pltpu.HBM(half, bf16),
            pltpu.HBM(half, bf16),
            pltpu.HBM((row_count, hidden_units), bf16),
            pltpu.HBM((row_count, 2 * hidden_units), bf16),
        ],
        scratch_shapes=[
            pltpu.VMEM((2, row_count, width), bf16),
            pltpu.VMEM((2, row_count, width), bf16),
            pltpu.VMEM(weight_dn.shape, bf16),
            pltpu.VMEM((row_count, hidden_units), bf16),
            pltpu.VMEM((2, row_count, 2 * hidden_units), bf16),
            pltpu.VMEM((group_count, 2 * capacity, width), bf16),
            pltpu.VMEM((group_count, token_count, width), bf16),
            pltpu.SemaphoreType.DMA((10 + 2 * (hidden_units // tile) + group_count,)),
        ],
        compiler_params=kernel_params(shared_vmem_bytes),
        cost_estimate=light(),
        name="backward_rows",
    )(which, gates.reshape(-1, token_count), *map(in_main, (keep_c, keep_h, *give)), in_vector(weight_gu), in_main(weight_dn))


def forward_kernel(
    capacity, gates_ref, tokens_ref, gu_ref, dn_ref, out_ref,
    tokens, gu, dn, rows, scales, hidden, o, sums, sems,
):
    group_count, _, width = tokens.shape
    hidden_units = dn.shape[1]
    row_count = group_count * capacity
    copies = Copies(sems)
    for group in range(group_count):
        copies.start(("tokens", group), tokens_ref.at[group], tokens.at[group])
    for expert in range(2):
        weight_copies(copies, expert, expert, gu_ref, dn_ref, gu, dn)
    gates = gates_ref[...]
    rank = ranks(gates)
    for group in range(group_count):
        onehot = onehot_rows(rank, group, 2, capacity)
        scale = slot_gates(onehot, gates, group, 2, capacity)
        copies.wait(("tokens", group))
        placed = dot(onehot.astype(jnp.bfloat16), tokens[group]).astype(jnp.bfloat16)
        here = slice(group * capacity, (group + 1) * capacity)
        for expert in range(2):
            own = slice(expert * capacity, (expert + 1) * capacity)
            rows[expert, here] = placed[own]
            scales[expert, here] = jnp.broadcast_to(scale[own], (capacity, 128))
    for expert in range(2):
        for start in range(0, hidden_units, tile):
            cols = slice(start, start + tile)
            up_cols = slice(hidden_units + start, hidden_units + start + tile)
            copies.wait(("gu", expert, start))
            gate_pre = dot(rows[expert], gu[expert, :, cols])
            up_pre = dot(rows[expert], gu[expert, :, up_cols])
            hidden[:, cols] = (gate_pre / (1.0 + jnp.exp(-gate_pre)) * up_pre).astype(jnp.bfloat16)
        for start in range(0, hidden_units, tile):
            copies.wait(("dn", expert, start))
        scale = scales[expert][:, :1]
        for start in range(0, width, tile):
            cols = slice(start, start + tile)
            part = (dot(hidden[...], dn[expert, :, cols]) * scale).astype(jnp.bfloat16)
            o[:, expert * capacity : (expert + 1) * capacity, cols] = part.reshape(
                group_count, capacity, tile
            )

    def store(group, value):
        sums[group] = value
        copies.start("out", sums.at[group], out_ref.at[group])

    combine(gates, o, capacity, store)
    copies.wait_all()


def forward_rows(tokens, gates, weight_gu, weight_dn, capacity):
    group_count, token_count, width = tokens.shape
    hidden_units = weight_dn.shape[1]
    row_count = group_count * capacity
    tiles = hidden_units // tile
    bf16 = jnp.bfloat16
    return pl.pallas_call(
        functools.partial(forward_kernel, capacity),
        in_specs=[vector] + [anywhere] * 3,
        out_specs=anywhere,
        out_shape=jax.ShapeDtypeStruct((group_count, token_count, width), bf16),
        scratch_shapes=[
            pltpu.VMEM((group_count, token_count, width), bf16),
            pltpu.VMEM(weight_gu.shape, bf16),
            pltpu.VMEM(weight_dn.shape, bf16),
            pltpu.VMEM((2, row_count, width), bf16),
            pltpu.VMEM((2, row_count, 128), jnp.float32),
            pltpu.VMEM((row_count, hidden_units), bf16),
            pltpu.VMEM((group_count, 2 * capacity, width), bf16),
            pltpu.VMEM((group_count, token_count, width), bf16),
            pltpu.SemaphoreType.DMA((6 * tiles + 2 * group_count,)),
        ],
        compiler_params=kernel_params(),
        cost_estimate=light(),
        name="forward_rows",
    )(gates.reshape(-1, token_count), tokens, weight_gu, weight_dn)


def gradient_kernel(near_rows, send_count, which_ref, *refs):
    before, refs = refs[: 4 if near_rows else 2], refs[4 if near_rows else 2 :]
    sends, refs = refs[:send_count], refs[send_count:]
    gu_ref, dn_ref, gu_out, dn_out, c, h, hidden, d, gu, dn, gu_sums, dn_sums, sems = refs
    row_count, width = c.shape
    hidden_units = dn.shape[1]
    near = slice(0, near_rows)
    far = slice(near_rows, row_count)
    copies = Copies(sems)
    start = near_rows
    for send in sends:
        place = slice(start, start + send.shape[1])
        start = place.stop
        copies.start("far", send.at[1], h.at[place])
        copies.start("far", send.at[0], c.at[place])
    weight_copies(copies, 0, which_ref[0], gu_ref, dn_ref, gu, dn)
    if near_rows:
        copies.start("dn sums", before[2], hidden.at[near])
        copies.start("dn sums", before[0], c.at[near])
        copies.start("gu sums", before[3], d.at[near])
        copies.start("gu sums", before[1], h.at[near])
    else:
        copies.start("dn sums", before[1], dn_sums)
        copies.start("gu sums", before[0], gu_sums)
    copies.wait("far")
    hidden_gradients(
        copies, 0, lambda: h[far], lambda: c[far], gu.at[0], dn.at[0], hidden.at[far], d.at[far]
    )

    def accumulate(name, left, right, sums, out):
        copies.wait(name)
        for start in range(0, left.shape[1], tile):
            cols = slice(start, start + tile)
            total = dot(left[:, cols], right[...], ((0,), (0,)))
            if not near_rows:
                total = total + sums[cols].astype(jnp.float32)
            sums[cols] = total.astype(jnp.bfloat16)
            copies.start("out", sums.at[cols], out.at[cols])

    accumulate("dn sums", hidden, c, dn_sums, dn_out)
    accumulate("gu sums", h, d, gu_sums, gu_out)
    copies.wait_all()


def weight_gradients(which, before, sends, weight_gu, weight_dn):
    width = weight_gu.shape[1]
    hidden_units = weight_dn.shape[1]
    near_rows = before[0].shape[0] if len(before) == 4 else 0
    row_count = near_rows + sum(send.shape[1] for send in sends)
    bf16 = jnp.bfloat16
    gu_shape = (width, 2 * hidden_units)
    dn_shape = (hidden_units, width)
    count = 2 * len(sends) + len(before) + 4 * (hidden_units // tile) + width // tile
    return pl.pallas_call(
        functools.partial(gradient_kernel, near_rows, len(sends)),
        in_specs=[scalar] + [anywhere] * (len(before) + len(sends) + 2),
        out_specs=[anywhere] * 2,
        out_shape=[jax.ShapeDtypeStruct(gu_shape, bf16), jax.ShapeDtypeStruct(dn_shape, bf16)],
        scratch_shapes=[
            pltpu.VMEM((row_count, width), bf16),
            pltpu.VMEM((row_count, width), bf16),
            pltpu.VMEM((row_count, hidden_units), bf16),
            pltpu.VMEM((row_count, 2 * hidden_units), bf16),
            pltpu.VMEM((1,) + gu_shape, bf16),
            pltpu.VMEM((1,) + dn_shape, bf16),
            pltpu.VMEM(gu_shape, bf16),
            pltpu.VMEM(dn_shape, bf16),
            pltpu.SemaphoreType.DMA((count,)),
        ],
        compiler_params=kernel_params(),
        cost_estimate=light(),
        name="weight_gradients",
    )(which, *before, *sends, weight_gu, weight_dn)


def swap_cores(value):
    return lax.ppermute(value, "expert", [(i, i ^ 1) for i in range(lax.axis_size("expert"))])


def exchange_sums(chip):
    group_count = lax.axis_size("expert")
    lines = [list(range(c, group_count, 2)) for c in range(2)]
    return lax.all_to_all(
        chip, "expert", split_axis=0, concat_axis=0, tiled=True, axis_index_groups=lines
    )


def per_device(
    x_fwd, gate_fwd, route_fwd, x_bwd, gate_bwd, route_bwd, cotangent, norm_gain, w_gate_up, w_down
):
    group_count = lax.axis_size("expert")
    section_count = lax.axis_size("pipe")
    local_count = w_gate_up.shape[1]
    expert_count = local_count * group_count
    token_count, model_width = x_fwd.shape
    pick_count = route_fwd.shape[1]
    capacity = token_count * pick_count * 4 // (3 * expert_count)
    weight_gu = w_gate_up[0]
    weight_dn = w_down[0]

    upper_half = (lax.axis_index("pipe") >= section_count // 2).astype(jnp.int32)
    which = jnp.stack([upper_half, 1 - upper_half])
    core = lax.axis_index("expert") % 2
    chips = 2 * jnp.arange(group_count // 2, dtype=jnp.int32)
    order = jnp.concatenate([chips + core, chips + 1 - core])
    sides = jnp.stack([core, 1 - core])

    send_gates = jnp.stack(
        [
            expert_gates(gate_fwd, route_fwd, expert_count),
            expert_gates(gate_bwd, route_bwd, expert_count),
        ]
    ).reshape(2, group_count, local_count, token_count)
    recv_gates = lax.all_to_all(
        send_gates.transpose(1, 0, 2, 3), "expert", split_axis=0, concat_axis=0, tiled=True
    )
    gates_f = recv_gates[:, 0]
    gates_b = recv_gates[:, 1][order][:, which]
    gathered_bwd = lax.all_gather(
        normed(x_bwd, norm_gain, cotangent)[None], "expert", axis=0, tiled=True
    )
    gathered_fwd = lax.all_gather(normed(x_fwd, norm_gain), "expert", axis=0, tiled=True)

    mirror = [(i, section_count - 1 - i) for i in range(section_count)]
    keep_c, keep_h, *give = place_rows(gathered_bwd, gates_b, sides, capacity)
    far = [lax.ppermute(part, "pipe", mirror) for part in give]

    own_dh, other_dh, keep_hidden, keep_d = backward_rows(
        keep_c, keep_h, give, weight_gu, weight_dn, gates_b, which, capacity
    )
    other_dh, far[0] = lax.optimization_barrier((other_dh, far[0]))
    other_dh = swap_cores(other_dh)
    middle = token_count // 2
    chip_dh = [
        (own_dh[:, part].astype(jnp.float32) + other_dh[:, part].astype(jnp.float32)).astype(
            jnp.bfloat16
        )
        for part in (slice(0, middle), slice(middle, token_count))
    ]
    parts_dh = [exchange_sums(chip) for chip in chip_dh]

    partial_y = forward_rows(gathered_fwd, gates_f, weight_gu, weight_dn, capacity)
    partial_y, parts_dh[0], far[1] = lax.optimization_barrier((partial_y, parts_dh[0], far[1]))
    y_fwd = lax.psum_scatter(
        partial_y.reshape(group_count * token_count, model_width),
        "expert",
        scatter_dimension=0,
        tiled=True,
    )

    dh_sum = jnp.concatenate([jnp.sum(part.astype(jnp.float32), axis=0) for part in parts_dh])
    bwd_hat, bwd_scale = normalize(x_bwd)
    scaled_dh = norm_gain * dh_sum
    dx_bwd = (
        bwd_scale * (scaled_dh - bwd_hat * jnp.mean(bwd_hat * scaled_dh, axis=-1, keepdims=True))
    ).astype(jnp.bfloat16)

    dx_bwd, far[2] = lax.optimization_barrier((dx_bwd, far[2]))
    gradients = weight_gradients(
        which, (keep_c, keep_h, keep_hidden, keep_d), far[:2], weight_gu, weight_dn
    )
    out_gu, out_dn = weight_gradients(which, gradients, far[2:], weight_gu, weight_dn)
    return (y_fwd, dx_bwd, out_gu[None, None], out_dn[None, None])


def solution(mesh):
    rows = P(("pipe", "expert"), None)
    experts = P("pipe", "expert", None, None)
    return jax.shard_map(
        per_device,
        mesh=mesh,
        in_specs=(rows,) * 7 + (P(), experts, experts),
        out_specs=(rows, rows, experts, experts),
        check_vma=False,
    )
```

```python
import functools

import jax
import jax.numpy as jnp
from jax import lax
from jax.experimental import pallas as pl
from jax.experimental.pallas import tpu as pltpu
from jax.sharding import PartitionSpec as P

norm_eps = 1e-06
tile = 256
vmem_bytes = 56 * 1024 * 1024
shared_vmem_bytes = 28 * 1024 * 1024


def params():
    return pltpu.CompilerParams(
        dimension_semantics=("arbitrary",), vmem_limit_bytes=shared_vmem_bytes
    )


def light():
    return pl.CostEstimate(flops=1000, bytes_accessed=1000, transcendentals=0)


def dot(a, b, contract=((1,), (0,))):
    return lax.dot_general(a, b, (contract, ((), ())), preferred_element_type=jnp.float32)


def normalize(inputs):
    values = inputs.astype(jnp.float32)
    scale = lax.rsqrt(jnp.mean(values * values, axis=-1, keepdims=True) + norm_eps)
    return (values * scale, scale)


def norm_kernel(x_ref, gain_ref, *refs):
    out_ref = refs[-1]
    values = x_ref[...].astype(jnp.float32)
    scale = lax.rsqrt(jnp.mean(values * values, axis=-1, keepdims=True) + norm_eps)
    out_ref[len(refs) - 1] = (values * scale * gain_ref[...][None, :]).astype(jnp.bfloat16)
    for index, other_ref in enumerate(refs[:-1]):
        out_ref[index] = other_ref[...]


def normed(x, gain, *others):
    return pl.pallas_call(
        norm_kernel,
        out_shape=jax.ShapeDtypeStruct((1 + len(others),) + x.shape, jnp.bfloat16),
        cost_estimate=light(),
        name="normed",
    )(x, gain, *others)


def expert_gates(gates, routes, expert_count):
    chosen = routes[None, :, :] == jnp.arange(expert_count, dtype=jnp.int32)[:, None, None]
    return jnp.sum(jnp.where(chosen, gates[None], 0.0), axis=-1)


def ranks(gates):
    named = gates > 0.0
    token_count = gates.shape[1]
    upto = lax.broadcasted_iota(jnp.int32, (token_count, token_count), 0) <= (
        lax.broadcasted_iota(jnp.int32, (token_count, token_count), 1)
    )
    count = dot(
        jnp.where(named, 1.0, 0.0).astype(jnp.bfloat16), jnp.where(upto, 1.0, 0.0).astype(jnp.bfloat16)
    )
    return jnp.where(named, count - 1.0, -1.0)


def onehot_rows(rank, group, local_count, capacity):
    token_count = rank.shape[1]
    slots = lax.broadcasted_iota(jnp.int32, (capacity, token_count), 0).astype(jnp.float32)
    parts = []
    for local in range(local_count):
        row = group * local_count + local
        parts.append(jnp.where(rank[row : row + 1, :] == slots, 1.0, 0.0))
    return jnp.concatenate(parts, axis=0)


def slot_gates(onehot, gates, group, local_count, capacity):
    parts = []
    for local in range(local_count):
        row = group * local_count + local
        own = onehot[local * capacity : (local + 1) * capacity]
        parts.append(jnp.sum(own * gates[row : row + 1, :], axis=1, keepdims=True))
    return jnp.concatenate(parts, axis=0)


def cuts(row_count):
    ends = [0, row_count * 9 // 32, row_count // 2, row_count]
    return [(start, end) for start, end in zip(ends[:-1], ends[1:])]


def overlaps(row_count, start, end):
    for send, (low, high) in enumerate(cuts(row_count)):
        first, last = max(start, low), min(end, high)
        if first < last:
            yield send, slice(first - low, last - low), slice(first - start, last - start)


def place_kernel(
    capacity, sides_ref, c_ref, h_ref, gates_ref, keep_c_ref, keep_h_ref, *give_refs
):
    half = h_ref.shape[0]
    row_count = 2 * half * capacity

    def place(side):
        gates = gates_ref[0]
        rank = ranks(gates)
        for group in range(half):
            onehot = onehot_rows(rank, group, 2, capacity)
            scale = slot_gates(onehot, gates, group, 2, capacity)
            onehot = onehot.astype(jnp.bfloat16)
            rows_c = (dot(onehot, c_ref[group, 0, 0]) * scale).astype(jnp.bfloat16)
            rows_h = dot(onehot, h_ref[group, 0, 0]).astype(jnp.bfloat16)
            here = slice(group * capacity, (group + 1) * capacity)
            keep_c_ref[here] = rows_c[:capacity]
            keep_h_ref[here] = rows_h[:capacity]
            first = (side * half + group) * capacity
            for send, there, part in overlaps(row_count, first, first + capacity):
                give_refs[send][0, there] = rows_c[capacity:][part]
                give_refs[send][1, there] = rows_h[capacity:][part]

    for side in range(2):
        pl.when(pl.program_id(0) == side)(functools.partial(place, side))


def in_main(value):
    return pltpu.with_memory_space_constraint(value, pltpu.HBM)


def place_rows(tokens, gates, sides, capacity):
    group_count, _, token_count, width = tokens.shape
    half = group_count // 2
    row_count = group_count * capacity
    rows_spec = pl.BlockSpec((row_count // 2, width), lambda i, sides: (i, 0))
    give_shapes = [(2, end - start, width) for start, end in cuts(row_count)]
    block = (half, 1, 1, token_count, width)
    tokens = tokens.reshape(half, 2, 2, token_count, width)
    return pl.pallas_call(
        functools.partial(place_kernel, capacity),
        grid_spec=pltpu.PrefetchScalarGridSpec(
            num_scalar_prefetch=1,
            grid=(2,),
            in_specs=[
                pl.BlockSpec(block, lambda i, sides: (0, sides[i], 0, 0, 0)),
                pl.BlockSpec(block, lambda i, sides: (0, sides[i], 1, 0, 0)),
                pl.BlockSpec((1, half * 2, token_count), lambda i, sides: (i, 0, 0)),
            ],
            out_specs=[rows_spec, rows_spec]
            + [pl.BlockSpec(shape, lambda i, sides: (0, 0, 0)) for shape in give_shapes],
        ),
        out_shape=[pltpu.HBM((row_count, width), jnp.bfloat16)] * 2
        + [pltpu.HBM(shape, jnp.bfloat16) for shape in give_shapes],
        compiler_params=params(),
        cost_estimate=light(),
        name="place_rows",
    )(sides, in_main(tokens), in_main(tokens), gates.reshape(2, half * 2, token_count))


class Copies:
    def __init__(self, sems):
        self.sems = sems
        self.count = 0
        self.waiting = {}

    def start(self, name, source, target):
        copy = pltpu.make_async_copy(source, target, self.sems.at[self.count])
        self.count += 1
        copy.start()
        self.waiting.setdefault(name, []).append(copy)

    def wait(self, name):
        for copy in self.waiting.pop(name, []):
            copy.wait()

    def wait_all(self):
        for name in list(self.waiting):
            self.wait(name)


def weight_copies(copies, expert, source, gu_ref, dn_ref, gu, dn):
    hidden_units = dn.shape[1]
    for start in range(0, hidden_units, tile):
        for base in (0, hidden_units):
            cols = slice(base + start, base + start + tile)
            copies.start(("gu", expert, start), gu_ref.at[source, :, cols], gu.at[expert, :, cols])
        rows = slice(start, start + tile)
        copies.start(("dn", expert, start), dn_ref.at[source, rows], dn.at[expert, rows])


def down_copies(copies, expert, source, dn_ref, dn):
    for start in range(0, dn.shape[1], tile):
        part = slice(start, start + tile)
        copies.start(("dn", expert, start), dn_ref.at[source, part], dn.at[expert, part])


def hidden_gradients(copies, key, h, c, gu, dn, hidden_ref, d_ref):
    hidden_units = dn.shape[0]
    for start in range(0, hidden_units, tile):
        cols = slice(start, start + tile)
        up_cols = slice(hidden_units + start, hidden_units + start + tile)
        copies.wait(("gu", key, start))
        gate_pre = dot(h(), gu[:, cols])
        up_pre = dot(h(), gu[:, up_cols])
        copies.wait("c%d" % key)
        copies.wait(("dn", key, start))
        back = dot(c(), dn[cols, :], ((1,), (1,)))
        squash = 1.0 / (1.0 + jnp.exp(-gate_pre))
        activated = gate_pre * squash
        if hidden_ref is not None:
            hidden_ref[:, cols] = (activated * up_pre).astype(jnp.bfloat16)
        d_ref[:, cols] = (back * up_pre * squash * (1.0 + gate_pre * (1.0 - squash))).astype(
            jnp.bfloat16
        )
        d_ref[:, up_cols] = (back * activated).astype(jnp.bfloat16)


anywhere = pl.BlockSpec(memory_space=pl.ANY)
vector = pl.BlockSpec(memory_space=pltpu.VMEM)
scalar = pl.BlockSpec(memory_space=pltpu.SMEM)


def in_vector(value):
    return pltpu.with_memory_space_constraint(value, pltpu.VMEM)


def kernel_params(limit=vmem_bytes):
    return pltpu.CompilerParams(vmem_limit_bytes=limit)


def combine(gates, rows_ref, capacity, store):
    rank = ranks(gates)
    for group in range(rows_ref.shape[0]):
        onehot = onehot_rows(rank, group, 2, capacity).T.astype(jnp.bfloat16)
        store(group, dot(onehot, rows_ref[group]).astype(jnp.bfloat16))


def backward_kernel(
    capacity, which_ref, gates_ref, keep_c_ref, keep_h_ref, give_1_ref, give_2_ref, give_3_ref,
    gu, dn_ref, own_ref, other_ref, hidden_out, d_out,
    c, h, dn, hidden, d, dh, sums, sems,
):
    row_count, width = keep_c_ref.shape
    group_count = row_count // capacity
    half = group_count // 2
    copies = Copies(sems)
    copies.start("h0", keep_h_ref, h.at[0])
    copies.start("c0", keep_c_ref, c.at[0])
    down_copies(copies, 0, which_ref[0], dn_ref, dn)
    copies.wait("h0")
    for send, there, part in overlaps(row_count, 0, row_count):
        give_ref = (give_1_ref, give_2_ref, give_3_ref)[send]
        copies.start("c1", give_ref.at[0, there], c.at[1, part])
        copies.start("h1", give_ref.at[1, there], h.at[1, part])
    down_copies(copies, 1, which_ref[1], dn_ref, dn)
    for expert in range(2):
        source = which_ref[expert]
        copies.wait("h%d" % expert)
        hidden_gradients(
            copies,
            expert,
            lambda: h[expert],
            lambda: c[expert],
            gu.at[source],
            dn.at[expert],
            hidden if expert == 0 else None,
            d.at[expert],
        )
        if expert == 0:
            copies.start("out", hidden, hidden_out)
            copies.start("out", d.at[0], d_out)
        for start in range(0, width, tile):
            cols = slice(start, start + tile)
            part = dot(d[expert], gu[source, cols, :], ((1,), (1,))).astype(jnp.bfloat16)
            dh[:, expert * capacity : (expert + 1) * capacity, cols] = part.reshape(
                group_count, capacity, tile
            )

    def store(group, value):
        sums[group] = value
        target = own_ref if group < half else other_ref
        copies.start("out", sums.at[group], target.at[group % half])

    combine(gates_ref[...], dh, capacity, store)
    copies.wait_all()


def backward_rows(keep_c, keep_h, give, weight_gu, weight_dn, gates, which, capacity):
    row_count, width = keep_c.shape
    hidden_units = weight_dn.shape[1]
    group_count = row_count // capacity
    token_count = gates.shape[-1]
    half = (group_count // 2, token_count, width)
    bf16 = jnp.bfloat16
    return pl.pallas_call(
        functools.partial(backward_kernel, capacity),
        in_specs=[scalar, vector] + [anywhere] * 5 + [vector, anywhere],
        out_specs=[anywhere] * 4,
        out_shape=[
            pltpu.HBM(half, bf16),
            pltpu.HBM(half, bf16),
            pltpu.HBM((row_count, hidden_units), bf16),
            pltpu.HBM((row_count, 2 * hidden_units), bf16),
        ],
        scratch_shapes=[
            pltpu.VMEM((2, row_count, width), bf16),
            pltpu.VMEM((2, row_count, width), bf16),
            pltpu.VMEM(weight_dn.shape, bf16),
            pltpu.VMEM((row_count, hidden_units), bf16),
            pltpu.VMEM((2, row_count, 2 * hidden_units), bf16),
            pltpu.VMEM((group_count, 2 * capacity, width), bf16),
            pltpu.VMEM((group_count, token_count, width), bf16),
            pltpu.SemaphoreType.DMA((10 + 2 * (hidden_units // tile) + group_count,)),
        ],
        compiler_params=kernel_params(shared_vmem_bytes),
        cost_estimate=light(),
        name="backward_rows",
    )(which, gates.reshape(-1, token_count), *map(in_main, (keep_c, keep_h, *give)), in_vector(weight_gu), in_main(weight_dn))


def forward_kernel(
    capacity, gates_ref, tokens_ref, gu_ref, dn_ref, out_ref,
    tokens, gu, dn, rows, scales, hidden, o, sums, sems,
):
    group_count, _, width = tokens.shape
    hidden_units = dn.shape[1]
    row_count = group_count * capacity
    copies = Copies(sems)
    for group in range(group_count):
        copies.start(("tokens", group), tokens_ref.at[group], tokens.at[group])
    for expert in range(2):
        weight_copies(copies, expert, expert, gu_ref, dn_ref, gu, dn)
    gates = gates_ref[...]
    rank = ranks(gates)
    for group in range(group_count):
        onehot = onehot_rows(rank, group, 2, capacity)
        scale = slot_gates(onehot, gates, group, 2, capacity)
        copies.wait(("tokens", group))
        placed = dot(onehot.astype(jnp.bfloat16), tokens[group]).astype(jnp.bfloat16)
        here = slice(group * capacity, (group + 1) * capacity)
        for expert in range(2):
            own = slice(expert * capacity, (expert + 1) * capacity)
            rows[expert, here] = placed[own]
            scales[expert, here] = jnp.broadcast_to(scale[own], (capacity, 128))
    for expert in range(2):
        for start in range(0, hidden_units, tile):
            cols = slice(start, start + tile)
            up_cols = slice(hidden_units + start, hidden_units + start + tile)
            copies.wait(("gu", expert, start))
            gate_pre = dot(rows[expert], gu[expert, :, cols])
            up_pre = dot(rows[expert], gu[expert, :, up_cols])
            hidden[:, cols] = (gate_pre / (1.0 + jnp.exp(-gate_pre)) * up_pre).astype(jnp.bfloat16)
        for start in range(0, hidden_units, tile):
            copies.wait(("dn", expert, start))
        scale = scales[expert][:, :1]
        for start in range(0, width, tile):
            cols = slice(start, start + tile)
            part = (dot(hidden[...], dn[expert, :, cols]) * scale).astype(jnp.bfloat16)
            o[:, expert * capacity : (expert + 1) * capacity, cols] = part.reshape(
                group_count, capacity, tile
            )

    def store(group, value):
        sums[group] = value
        copies.start("out", sums.at[group], out_ref.at[group])

    combine(gates, o, capacity, store)
    copies.wait_all()


def forward_rows(tokens, gates, weight_gu, weight_dn, capacity):
    group_count, token_count, width = tokens.shape
    hidden_units = weight_dn.shape[1]
    row_count = group_count * capacity
    tiles = hidden_units // tile
    bf16 = jnp.bfloat16
    return pl.pallas_call(
        functools.partial(forward_kernel, capacity),
        in_specs=[vector] + [anywhere] * 3,
        out_specs=anywhere,
        out_shape=jax.ShapeDtypeStruct((group_count, token_count, width), bf16),
        scratch_shapes=[
            pltpu.VMEM((group_count, token_count, width), bf16),
            pltpu.VMEM(weight_gu.shape, bf16),
            pltpu.VMEM(weight_dn.shape, bf16),
            pltpu.VMEM((2, row_count, width), bf16),
            pltpu.VMEM((2, row_count, 128), jnp.float32),
            pltpu.VMEM((row_count, hidden_units), bf16),
            pltpu.VMEM((group_count, 2 * capacity, width), bf16),
            pltpu.VMEM((group_count, token_count, width), bf16),
            pltpu.SemaphoreType.DMA((6 * tiles + 2 * group_count,)),
        ],
        compiler_params=kernel_params(),
        cost_estimate=light(),
        name="forward_rows",
    )(gates.reshape(-1, token_count), tokens, weight_gu, weight_dn)


def gradient_kernel(near_rows, send_count, which_ref, *refs):
    before, refs = refs[: 4 if near_rows else 2], refs[4 if near_rows else 2 :]
    sends, refs = refs[:send_count], refs[send_count:]
    gu_ref, dn_ref, gu_out, dn_out, c, h, hidden, d, gu, dn, gu_sums, dn_sums, sems = refs
    row_count, width = c.shape
    hidden_units = dn.shape[1]
    near = slice(0, near_rows)
    far = slice(near_rows, row_count)
    copies = Copies(sems)
    start = near_rows
    for send in sends:
        place = slice(start, start + send.shape[1])
        start = place.stop
        copies.start("far", send.at[1], h.at[place])
        copies.start("far", send.at[0], c.at[place])
    weight_copies(copies, 0, which_ref[0], gu_ref, dn_ref, gu, dn)
    if near_rows:
        copies.start("dn sums", before[2], hidden.at[near])
        copies.start("dn sums", before[0], c.at[near])
        copies.start("gu sums", before[3], d.at[near])
        copies.start("gu sums", before[1], h.at[near])
    else:
        copies.start("dn sums", before[1], dn_sums)
        copies.start("gu sums", before[0], gu_sums)
    copies.wait("far")
    hidden_gradients(
        copies, 0, lambda: h[far], lambda: c[far], gu.at[0], dn.at[0], hidden.at[far], d.at[far]
    )

    def accumulate(name, left, right, sums, out):
        copies.wait(name)
        for start in range(0, left.shape[1], tile):
            cols = slice(start, start + tile)
            total = dot(left[:, cols], right[...], ((0,), (0,)))
            if not near_rows:
                total = total + sums[cols].astype(jnp.float32)
            sums[cols] = total.astype(jnp.bfloat16)
            copies.start("out", sums.at[cols], out.at[cols])

    accumulate("dn sums", hidden, c, dn_sums, dn_out)
    accumulate("gu sums", h, d, gu_sums, gu_out)
    copies.wait_all()


def weight_gradients(which, before, sends, weight_gu, weight_dn):
    width = weight_gu.shape[1]
    hidden_units = weight_dn.shape[1]
    near_rows = before[0].shape[0] if len(before) == 4 else 0
    row_count = near_rows + sum(send.shape[1] for send in sends)
    bf16 = jnp.bfloat16
    gu_shape = (width, 2 * hidden_units)
    dn_shape = (hidden_units, width)
    count = 2 * len(sends) + len(before) + 4 * (hidden_units // tile) + width // tile
    return pl.pallas_call(
        functools.partial(gradient_kernel, near_rows, len(sends)),
        in_specs=[scalar] + [anywhere] * (len(before) + len(sends) + 2),
        out_specs=[anywhere] * 2,
        out_shape=[jax.ShapeDtypeStruct(gu_shape, bf16), jax.ShapeDtypeStruct(dn_shape, bf16)],
        scratch_shapes=[
            pltpu.VMEM((row_count, width), bf16),
            pltpu.VMEM((row_count, width), bf16),
            pltpu.VMEM((row_count, hidden_units), bf16),
            pltpu.VMEM((row_count, 2 * hidden_units), bf16),
            pltpu.VMEM((1,) + gu_shape, bf16),
            pltpu.VMEM((1,) + dn_shape, bf16),
            pltpu.VMEM(gu_shape, bf16),
            pltpu.VMEM(dn_shape, bf16),
            pltpu.SemaphoreType.DMA((count,)),
        ],
        compiler_params=kernel_params(),
        cost_estimate=light(),
        name="weight_gradients",
    )(which, *before, *sends, weight_gu, weight_dn)


def swap_cores(value):
    return lax.ppermute(value, "expert", [(i, i ^ 1) for i in range(lax.axis_size("expert"))])


def exchange_sums(chip):
    group_count = lax.axis_size("expert")
    lines = [list(range(c, group_count, 2)) for c in range(2)]
    return lax.all_to_all(
        chip, "expert", split_axis=0, concat_axis=0, tiled=True, axis_index_groups=lines
    )


def per_device(
    x_fwd, gate_fwd, route_fwd, x_bwd, gate_bwd, route_bwd, cotangent, norm_gain, w_gate_up, w_down
):
    group_count = lax.axis_size("expert")
    section_count = lax.axis_size("pipe")
    local_count = w_gate_up.shape[1]
    expert_count = local_count * group_count
    token_count, model_width = x_fwd.shape
    pick_count = route_fwd.shape[1]
    capacity = token_count * pick_count * 4 // (3 * expert_count)
    weight_gu = w_gate_up[0]
    weight_dn = w_down[0]

    upper_half = (lax.axis_index("pipe") >= section_count // 2).astype(jnp.int32)
    which = jnp.stack([upper_half, 1 - upper_half])
    core = lax.axis_index("expert") % 2
    chips = 2 * jnp.arange(group_count // 2, dtype=jnp.int32)
    order = jnp.concatenate([chips + core, chips + 1 - core])
    sides = jnp.stack([core, 1 - core])

    send_gates = jnp.stack(
        [
            expert_gates(gate_fwd, route_fwd, expert_count),
            expert_gates(gate_bwd, route_bwd, expert_count),
        ]
    ).reshape(2, group_count, local_count, token_count)
    recv_gates = lax.all_to_all(
        send_gates.transpose(1, 0, 2, 3), "expert", split_axis=0, concat_axis=0, tiled=True
    )
    gates_f = recv_gates[:, 0]
    gates_b = recv_gates[:, 1][order][:, which]
    gathered_bwd = lax.all_gather(
        normed(x_bwd, norm_gain, cotangent)[None], "expert", axis=0, tiled=True
    )
    gathered_fwd = lax.all_gather(normed(x_fwd, norm_gain), "expert", axis=0, tiled=True)

    mirror = [(i, section_count - 1 - i) for i in range(section_count)]
    keep_c, keep_h, *give = place_rows(gathered_bwd, gates_b, sides, capacity)
    far = [lax.ppermute(part, "pipe", mirror) for part in give]

    own_dh, other_dh, keep_hidden, keep_d = backward_rows(
        keep_c, keep_h, give, weight_gu, weight_dn, gates_b, which, capacity
    )
    other_dh, far[0] = lax.optimization_barrier((other_dh, far[0]))
    other_dh = swap_cores(other_dh)
    middle = token_count // 2
    chip_dh = [
        (own_dh[:, part].astype(jnp.float32) + other_dh[:, part].astype(jnp.float32)).astype(
            jnp.bfloat16
        )
        for part in (slice(0, middle), slice(middle, token_count))
    ]
    parts_dh = [exchange_sums(chip) for chip in chip_dh]

    partial_y = forward_rows(gathered_fwd, gates_f, weight_gu, weight_dn, capacity)
    partial_y, parts_dh[0], far[1] = lax.optimization_barrier((partial_y, parts_dh[0], far[1]))
    y_fwd = lax.psum_scatter(
        partial_y.reshape(group_count * token_count, model_width),
        "expert",
        scatter_dimension=0,
        tiled=True,
    )

    dh_sum = jnp.concatenate([jnp.sum(part.astype(jnp.float32), axis=0) for part in parts_dh])
    bwd_hat, bwd_scale = normalize(x_bwd)
    scaled_dh = norm_gain * dh_sum
    dx_bwd = (
        bwd_scale * (scaled_dh - bwd_hat * jnp.mean(bwd_hat * scaled_dh, axis=-1, keepdims=True))
    ).astype(jnp.bfloat16)

    dx_bwd, far[2] = lax.optimization_barrier((dx_bwd, far[2]))
    gradients = weight_gradients(
        which, (keep_c, keep_h, keep_hidden, keep_d), far[:2], weight_gu, weight_dn
    )
    out_gu, out_dn = weight_gradients(which, gradients, far[2:], weight_gu, weight_dn)
    return (y_fwd, dx_bwd, out_gu[None, None], out_dn[None, None])


def solution(mesh):
    rows = P(("pipe", "expert"), None)
    experts = P("pipe", "expert", None, None)
    return jax.shard_map(
        per_device,
        mesh=mesh,
        in_specs=(rows,) * 7 + (P(), experts, experts),
        out_specs=(rows, rows, experts, experts),
        check_vma=False,
    )
```

```python
import functools

import jax
import jax.numpy as jnp
from jax import lax
from jax.experimental import pallas as pl
from jax.experimental.pallas import tpu as pltpu
from jax.sharding import PartitionSpec as P

norm_eps = 1e-06
tile = 256
vmem_bytes = 56 * 1024 * 1024
shared_vmem_bytes = 28 * 1024 * 1024


def params():
    return pltpu.CompilerParams(
        dimension_semantics=("arbitrary",), vmem_limit_bytes=shared_vmem_bytes
    )


def light():
    return pl.CostEstimate(flops=1000, bytes_accessed=1000, transcendentals=0)


def dot(a, b, contract=((1,), (0,))):
    return lax.dot_general(a, b, (contract, ((), ())), preferred_element_type=jnp.float32)


def normalize(inputs):
    values = inputs.astype(jnp.float32)
    scale = lax.rsqrt(jnp.mean(values * values, axis=-1, keepdims=True) + norm_eps)
    return (values * scale, scale)


def norm_kernel(x_ref, gain_ref, *refs):
    out_ref = refs[-1]
    values = x_ref[...].astype(jnp.float32)
    scale = lax.rsqrt(jnp.mean(values * values, axis=-1, keepdims=True) + norm_eps)
    out_ref[len(refs) - 1] = (values * scale * gain_ref[...][None, :]).astype(jnp.bfloat16)
    for index, other_ref in enumerate(refs[:-1]):
        out_ref[index] = other_ref[...]


def normed(x, gain, *others):
    return pl.pallas_call(
        norm_kernel,
        out_shape=jax.ShapeDtypeStruct((1 + len(others),) + x.shape, jnp.bfloat16),
        cost_estimate=light(),
        name="normed",
    )(x, gain, *others)


def expert_gates(gates, routes, expert_count):
    chosen = routes[None, :, :] == jnp.arange(expert_count, dtype=jnp.int32)[:, None, None]
    return jnp.sum(jnp.where(chosen, gates[None], 0.0), axis=-1)


def ranks(gates):
    named = gates > 0.0
    token_count = gates.shape[1]
    upto = lax.broadcasted_iota(jnp.int32, (token_count, token_count), 0) <= (
        lax.broadcasted_iota(jnp.int32, (token_count, token_count), 1)
    )
    count = dot(
        jnp.where(named, 1.0, 0.0).astype(jnp.bfloat16), jnp.where(upto, 1.0, 0.0).astype(jnp.bfloat16)
    )
    return jnp.where(named, count - 1.0, -1.0)


def onehot_rows(rank, group, local_count, capacity):
    token_count = rank.shape[1]
    slots = lax.broadcasted_iota(jnp.int32, (capacity, token_count), 0).astype(jnp.float32)
    parts = []
    for local in range(local_count):
        row = group * local_count + local
        parts.append(jnp.where(rank[row : row + 1, :] == slots, 1.0, 0.0))
    return jnp.concatenate(parts, axis=0)


def slot_gates(onehot, gates, group, local_count, capacity):
    parts = []
    for local in range(local_count):
        row = group * local_count + local
        own = onehot[local * capacity : (local + 1) * capacity]
        parts.append(jnp.sum(own * gates[row : row + 1, :], axis=1, keepdims=True))
    return jnp.concatenate(parts, axis=0)


def cuts(row_count):
    ends = [0, row_count * 9 // 32, row_count // 2, row_count]
    return [(start, end) for start, end in zip(ends[:-1], ends[1:])]


def overlaps(row_count, start, end):
    for send, (low, high) in enumerate(cuts(row_count)):
        first, last = max(start, low), min(end, high)
        if first < last:
            yield send, slice(first - low, last - low), slice(first - start, last - start)


def place_kernel(
    capacity, sides_ref, c_ref, h_ref, gates_ref, keep_c_ref, keep_h_ref, *give_refs
):
    half = h_ref.shape[0]
    row_count = 2 * half * capacity

    def place(side):
        gates = gates_ref[0]
        rank = ranks(gates)
        for group in range(half):
            onehot = onehot_rows(rank, group, 2, capacity)
            scale = slot_gates(onehot, gates, group, 2, capacity)
            onehot = onehot.astype(jnp.bfloat16)
            rows_c = (dot(onehot, c_ref[group, 0, 0]) * scale).astype(jnp.bfloat16)
            rows_h = dot(onehot, h_ref[group, 0, 0]).astype(jnp.bfloat16)
            here = slice(group * capacity, (group + 1) * capacity)
            keep_c_ref[here] = rows_c[:capacity]
            keep_h_ref[here] = rows_h[:capacity]
            first = (side * half + group) * capacity
            for send, there, part in overlaps(row_count, first, first + capacity):
                give_refs[send][0, there] = rows_c[capacity:][part]
                give_refs[send][1, there] = rows_h[capacity:][part]

    for side in range(2):
        pl.when(pl.program_id(0) == side)(functools.partial(place, side))


def in_main(value):
    return pltpu.with_memory_space_constraint(value, pltpu.HBM)


def place_rows(tokens, gates, sides, capacity):
    group_count, _, token_count, width = tokens.shape
    half = group_count // 2
    row_count = group_count * capacity
    rows_spec = pl.BlockSpec((row_count // 2, width), lambda i, sides: (i, 0))
    give_shapes = [(2, end - start, width) for start, end in cuts(row_count)]
    block = (half, 1, 1, token_count, width)
    tokens = tokens.reshape(half, 2, 2, token_count, width)
    return pl.pallas_call(
        functools.partial(place_kernel, capacity),
        grid_spec=pltpu.PrefetchScalarGridSpec(
            num_scalar_prefetch=1,
            grid=(2,),
            in_specs=[
                pl.BlockSpec(block, lambda i, sides: (0, sides[i], 0, 0, 0)),
                pl.BlockSpec(block, lambda i, sides: (0, sides[i], 1, 0, 0)),
                pl.BlockSpec((1, half * 2, token_count), lambda i, sides: (i, 0, 0)),
            ],
            out_specs=[rows_spec, rows_spec]
            + [pl.BlockSpec(shape, lambda i, sides: (0, 0, 0)) for shape in give_shapes],
        ),
        out_shape=[pltpu.HBM((row_count, width), jnp.bfloat16)] * 2
        + [pltpu.HBM(shape, jnp.bfloat16) for shape in give_shapes],
        compiler_params=params(),
        cost_estimate=light(),
        name="place_rows",
    )(sides, in_main(tokens), in_main(tokens), gates.reshape(2, half * 2, token_count))


class Copies:
    def __init__(self, sems):
        self.sems = sems
        self.count = 0
        self.waiting = {}

    def start(self, name, source, target):
        copy = pltpu.make_async_copy(source, target, self.sems.at[self.count])
        self.count += 1
        copy.start()
        self.waiting.setdefault(name, []).append(copy)

    def wait(self, name):
        for copy in self.waiting.pop(name, []):
            copy.wait()

    def wait_all(self):
        for name in list(self.waiting):
            self.wait(name)


def weight_copies(copies, expert, source, gu_ref, dn_ref, gu, dn):
    hidden_units = dn.shape[1]
    for start in range(0, hidden_units, tile):
        for base in (0, hidden_units):
            cols = slice(base + start, base + start + tile)
            copies.start(("gu", expert, start), gu_ref.at[source, :, cols], gu.at[expert, :, cols])
        rows = slice(start, start + tile)
        copies.start(("dn", expert, start), dn_ref.at[source, rows], dn.at[expert, rows])


def down_copies(copies, expert, source, dn_ref, dn):
    for start in range(0, dn.shape[1], tile):
        part = slice(start, start + tile)
        copies.start(("dn", expert, start), dn_ref.at[source, part], dn.at[expert, part])


def hidden_gradients(copies, key, h, c, gu, dn, hidden_ref, d_ref):
    hidden_units = dn.shape[0]
    for start in range(0, hidden_units, tile):
        cols = slice(start, start + tile)
        up_cols = slice(hidden_units + start, hidden_units + start + tile)
        copies.wait(("gu", key, start))
        gate_pre = dot(h(), gu[:, cols])
        up_pre = dot(h(), gu[:, up_cols])
        copies.wait("c%d" % key)
        copies.wait(("dn", key, start))
        back = dot(c(), dn[cols, :], ((1,), (1,)))
        squash = 1.0 / (1.0 + jnp.exp(-gate_pre))
        activated = gate_pre * squash
        if hidden_ref is not None:
            hidden_ref[:, cols] = (activated * up_pre).astype(jnp.bfloat16)
        d_ref[:, cols] = (back * up_pre * squash * (1.0 + gate_pre * (1.0 - squash))).astype(
            jnp.bfloat16
        )
        d_ref[:, up_cols] = (back * activated).astype(jnp.bfloat16)


anywhere = pl.BlockSpec(memory_space=pl.ANY)
vector = pl.BlockSpec(memory_space=pltpu.VMEM)
scalar = pl.BlockSpec(memory_space=pltpu.SMEM)


def in_vector(value):
    return pltpu.with_memory_space_constraint(value, pltpu.VMEM)


def kernel_params(limit=vmem_bytes):
    return pltpu.CompilerParams(vmem_limit_bytes=limit)


def combine(gates, rows_ref, capacity, store):
    rank = ranks(gates)
    for group in range(rows_ref.shape[0]):
        onehot = onehot_rows(rank, group, 2, capacity).T.astype(jnp.bfloat16)
        store(group, dot(onehot, rows_ref[group]).astype(jnp.bfloat16))


def token_halves(token_count):
    return (slice(0, token_count // 2), slice(token_count // 2, token_count))


def backward_kernel(
    capacity, which_ref, gates_ref, keep_c_ref, keep_h_ref, give_1_ref, give_2_ref, give_3_ref,
    gu, dn_ref, own_ref, other_1_ref, other_2_ref, hidden_out, d_out,
    c, h, dn, hidden, d, dh, sums, sems,
):
    row_count, width = keep_c_ref.shape
    group_count = row_count // capacity
    half = group_count // 2
    copies = Copies(sems)
    copies.start("h0", keep_h_ref, h.at[0])
    copies.start("c0", keep_c_ref, c.at[0])
    down_copies(copies, 0, which_ref[0], dn_ref, dn)
    copies.wait("h0")
    for send, there, part in overlaps(row_count, 0, row_count):
        give_ref = (give_1_ref, give_2_ref, give_3_ref)[send]
        copies.start("c1", give_ref.at[0, there], c.at[1, part])
        copies.start("h1", give_ref.at[1, there], h.at[1, part])
    down_copies(copies, 1, which_ref[1], dn_ref, dn)
    for expert in range(2):
        source = which_ref[expert]
        copies.wait("h%d" % expert)
        hidden_gradients(
            copies,
            expert,
            lambda: h[expert],
            lambda: c[expert],
            gu.at[source],
            dn.at[expert],
            hidden if expert == 0 else None,
            d.at[expert],
        )
        if expert == 0:
            copies.start("out", hidden, hidden_out)
            copies.start("out", d.at[0], d_out)
        for start in range(0, width, tile):
            cols = slice(start, start + tile)
            part = dot(d[expert], gu[source, cols, :], ((1,), (1,))).astype(jnp.bfloat16)
            dh[:, expert * capacity : (expert + 1) * capacity, cols] = part.reshape(
                group_count, capacity, tile
            )

    def store(group, value):
        sums[group] = value
        if group < half:
            copies.start("out", sums.at[group], own_ref.at[group])
        else:
            for part, target in zip(token_halves(sums.shape[1]), (other_1_ref, other_2_ref)):
                copies.start("out", sums.at[group, part], target.at[group - half])

    combine(gates_ref[...], dh, capacity, store)
    copies.wait_all()


def backward_rows(keep_c, keep_h, give, weight_gu, weight_dn, gates, which, capacity):
    row_count, width = keep_c.shape
    hidden_units = weight_dn.shape[1]
    group_count = row_count // capacity
    token_count = gates.shape[-1]
    half = (group_count // 2, token_count, width)
    quarter = (group_count // 2, token_count // 2, width)
    bf16 = jnp.bfloat16
    return pl.pallas_call(
        functools.partial(backward_kernel, capacity),
        in_specs=[scalar, vector] + [anywhere] * 5 + [vector, anywhere],
        out_specs=[anywhere] * 5,
        out_shape=[
            pltpu.HBM(half, bf16),
            pltpu.HBM(quarter, bf16),
            pltpu.HBM(quarter, bf16),
            pltpu.HBM((row_count, hidden_units), bf16),
            pltpu.HBM((row_count, 2 * hidden_units), bf16),
        ],
        scratch_shapes=[
            pltpu.VMEM((2, row_count, width), bf16),
            pltpu.VMEM((2, row_count, width), bf16),
            pltpu.VMEM(weight_dn.shape, bf16),
            pltpu.VMEM((row_count, hidden_units), bf16),
            pltpu.VMEM((2, row_count, 2 * hidden_units), bf16),
            pltpu.VMEM((group_count, 2 * capacity, width), bf16),
            pltpu.VMEM((group_count, token_count, width), bf16),
            pltpu.SemaphoreType.DMA((10 + 2 * (hidden_units // tile) + 3 * group_count // 2,)),
        ],
        compiler_params=kernel_params(shared_vmem_bytes),
        cost_estimate=light(),
        name="backward_rows",
    )(which, gates.reshape(-1, token_count), *map(in_main, (keep_c, keep_h, *give)), in_vector(weight_gu), in_main(weight_dn))


def forward_kernel(
    capacity, gates_ref, tokens_ref, gu_ref, dn_ref, out_ref,
    tokens, gu, dn, rows, scales, hidden, o, sums, sems,
):
    group_count, _, width = tokens.shape
    hidden_units = dn.shape[1]
    row_count = group_count * capacity
    copies = Copies(sems)
    for group in range(group_count):
        copies.start(("tokens", group), tokens_ref.at[group], tokens.at[group])
    for expert in range(2):
        weight_copies(copies, expert, expert, gu_ref, dn_ref, gu, dn)
    gates = gates_ref[...]
    rank = ranks(gates)
    for group in range(group_count):
        onehot = onehot_rows(rank, group, 2, capacity)
        scale = slot_gates(onehot, gates, group, 2, capacity)
        copies.wait(("tokens", group))
        placed = dot(onehot.astype(jnp.bfloat16), tokens[group]).astype(jnp.bfloat16)
        here = slice(group * capacity, (group + 1) * capacity)
        for expert in range(2):
            own = slice(expert * capacity, (expert + 1) * capacity)
            rows[expert, here] = placed[own]
            scales[expert, here] = jnp.broadcast_to(scale[own], (capacity, 128))
    for expert in range(2):
        for start in range(0, hidden_units, tile):
            cols = slice(start, start + tile)
            up_cols = slice(hidden_units + start, hidden_units + start + tile)
            copies.wait(("gu", expert, start))
            gate_pre = dot(rows[expert], gu[expert, :, cols])
            up_pre = dot(rows[expert], gu[expert, :, up_cols])
            hidden[:, cols] = (gate_pre / (1.0 + jnp.exp(-gate_pre)) * up_pre).astype(jnp.bfloat16)
        for start in range(0, hidden_units, tile):
            copies.wait(("dn", expert, start))
        scale = scales[expert][:, :1]
        for start in range(0, width, tile):
            cols = slice(start, start + tile)
            part = (dot(hidden[...], dn[expert, :, cols]) * scale).astype(jnp.bfloat16)
            o[:, expert * capacity : (expert + 1) * capacity, cols] = part.reshape(
                group_count, capacity, tile
            )

    def store(group, value):
        sums[group] = value
        copies.start("out", sums.at[group], out_ref.at[group])

    combine(gates, o, capacity, store)
    copies.wait_all()


def forward_rows(tokens, gates, weight_gu, weight_dn, capacity):
    group_count, token_count, width = tokens.shape
    hidden_units = weight_dn.shape[1]
    row_count = group_count * capacity
    tiles = hidden_units // tile
    bf16 = jnp.bfloat16
    return pl.pallas_call(
        functools.partial(forward_kernel, capacity),
        in_specs=[vector] + [anywhere] * 3,
        out_specs=anywhere,
        out_shape=jax.ShapeDtypeStruct((group_count, token_count, width), bf16),
        scratch_shapes=[
            pltpu.VMEM((group_count, token_count, width), bf16),
            pltpu.VMEM(weight_gu.shape, bf16),
            pltpu.VMEM(weight_dn.shape, bf16),
            pltpu.VMEM((2, row_count, width), bf16),
            pltpu.VMEM((2, row_count, 128), jnp.float32),
            pltpu.VMEM((row_count, hidden_units), bf16),
            pltpu.VMEM((group_count, 2 * capacity, width), bf16),
            pltpu.VMEM((group_count, token_count, width), bf16),
            pltpu.SemaphoreType.DMA((6 * tiles + 2 * group_count,)),
        ],
        compiler_params=kernel_params(),
        cost_estimate=light(),
        name="forward_rows",
    )(gates.reshape(-1, token_count), tokens, weight_gu, weight_dn)


def gradient_kernel(near_rows, send_count, which_ref, *refs):
    before, refs = refs[: 4 if near_rows else 2], refs[4 if near_rows else 2 :]
    sends, refs = refs[:send_count], refs[send_count:]
    gu_ref, dn_ref, gu_out, dn_out, c, h, hidden, d, gu, dn, gu_sums, dn_sums, sems = refs
    row_count, width = c.shape
    hidden_units = dn.shape[1]
    near = slice(0, near_rows)
    far = slice(near_rows, row_count)
    copies = Copies(sems)
    start = near_rows
    for send in sends:
        place = slice(start, start + send.shape[1])
        start = place.stop
        copies.start("far", send.at[1], h.at[place])
        copies.start("far", send.at[0], c.at[place])
    weight_copies(copies, 0, which_ref[0], gu_ref, dn_ref, gu, dn)
    if near_rows:
        copies.start("dn sums", before[2], hidden.at[near])
        copies.start("dn sums", before[0], c.at[near])
        copies.start("gu sums", before[3], d.at[near])
        copies.start("gu sums", before[1], h.at[near])
    else:
        copies.start("dn sums", before[1], dn_sums)
        copies.start("gu sums", before[0], gu_sums)
    copies.wait("far")
    hidden_gradients(
        copies, 0, lambda: h[far], lambda: c[far], gu.at[0], dn.at[0], hidden.at[far], d.at[far]
    )

    def accumulate(name, left, right, sums, out):
        copies.wait(name)
        for start in range(0, left.shape[1], tile):
            cols = slice(start, start + tile)
            total = dot(left[:, cols], right[...], ((0,), (0,)))
            if not near_rows:
                total = total + sums[cols].astype(jnp.float32)
            sums[cols] = total.astype(jnp.bfloat16)
            copies.start("out", sums.at[cols], out.at[cols])

    accumulate("dn sums", hidden, c, dn_sums, dn_out)
    accumulate("gu sums", h, d, gu_sums, gu_out)
    copies.wait_all()


def weight_gradients(which, before, sends, weight_gu, weight_dn):
    width = weight_gu.shape[1]
    hidden_units = weight_dn.shape[1]
    near_rows = before[0].shape[0] if len(before) == 4 else 0
    row_count = near_rows + sum(send.shape[1] for send in sends)
    bf16 = jnp.bfloat16
    gu_shape = (width, 2 * hidden_units)
    dn_shape = (hidden_units, width)
    count = 2 * len(sends) + len(before) + 4 * (hidden_units // tile) + width // tile
    return pl.pallas_call(
        functools.partial(gradient_kernel, near_rows, len(sends)),
        in_specs=[scalar] + [anywhere] * (len(before) + len(sends) + 2),
        out_specs=[anywhere] * 2,
        out_shape=[jax.ShapeDtypeStruct(gu_shape, bf16), jax.ShapeDtypeStruct(dn_shape, bf16)],
        scratch_shapes=[
            pltpu.VMEM((row_count, width), bf16),
            pltpu.VMEM((row_count, width), bf16),
            pltpu.VMEM((row_count, hidden_units), bf16),
            pltpu.VMEM((row_count, 2 * hidden_units), bf16),
            pltpu.VMEM((1,) + gu_shape, bf16),
            pltpu.VMEM((1,) + dn_shape, bf16),
            pltpu.VMEM(gu_shape, bf16),
            pltpu.VMEM(dn_shape, bf16),
            pltpu.SemaphoreType.DMA((count,)),
        ],
        compiler_params=kernel_params(),
        cost_estimate=light(),
        name="weight_gradients",
    )(which, *before, *sends, weight_gu, weight_dn)


def swap_cores(value):
    return lax.ppermute(value, "expert", [(i, i ^ 1) for i in range(lax.axis_size("expert"))])


def exchange_sums(chip):
    group_count = lax.axis_size("expert")
    lines = [list(range(c, group_count, 2)) for c in range(2)]
    return lax.all_to_all(
        chip, "expert", split_axis=0, concat_axis=0, tiled=True, axis_index_groups=lines
    )


def per_device(
    x_fwd, gate_fwd, route_fwd, x_bwd, gate_bwd, route_bwd, cotangent, norm_gain, w_gate_up, w_down
):
    group_count = lax.axis_size("expert")
    section_count = lax.axis_size("pipe")
    local_count = w_gate_up.shape[1]
    expert_count = local_count * group_count
    token_count, model_width = x_fwd.shape
    pick_count = route_fwd.shape[1]
    capacity = token_count * pick_count * 4 // (3 * expert_count)
    weight_gu = w_gate_up[0]
    weight_dn = w_down[0]

    upper_half = (lax.axis_index("pipe") >= section_count // 2).astype(jnp.int32)
    which = jnp.stack([upper_half, 1 - upper_half])
    core = lax.axis_index("expert") % 2
    chips = 2 * jnp.arange(group_count // 2, dtype=jnp.int32)
    order = jnp.concatenate([chips + core, chips + 1 - core])
    sides = jnp.stack([core, 1 - core])

    send_gates = jnp.stack(
        [
            expert_gates(gate_fwd, route_fwd, expert_count),
            expert_gates(gate_bwd, route_bwd, expert_count),
        ]
    ).reshape(2, group_count, local_count, token_count)
    recv_gates = lax.all_to_all(
        send_gates.transpose(1, 0, 2, 3), "expert", split_axis=0, concat_axis=0, tiled=True
    )
    gates_f = recv_gates[:, 0]
    gates_b = recv_gates[:, 1][order][:, which]
    gathered_bwd = lax.all_gather(
        normed(x_bwd, norm_gain, cotangent)[None], "expert", axis=0, tiled=True
    )
    gathered_fwd = lax.all_gather(normed(x_fwd, norm_gain), "expert", axis=0, tiled=True)

    mirror = [(i, section_count - 1 - i) for i in range(section_count)]
    keep_c, keep_h, *give = place_rows(gathered_bwd, gates_b, sides, capacity)
    far = [lax.ppermute(part, "pipe", mirror) for part in give]

    own_dh, *other_dh, keep_hidden, keep_d = backward_rows(
        keep_c, keep_h, give, weight_gu, weight_dn, gates_b, which, capacity
    )
    other_dh[0], far[0] = lax.optimization_barrier((other_dh[0], far[0]))
    parts_dh = []
    for part, other in zip(token_halves(token_count), other_dh):
        chip_dh = own_dh[:, part].astype(jnp.float32) + swap_cores(other).astype(jnp.float32)
        parts_dh.append(exchange_sums(chip_dh.astype(jnp.bfloat16)))

    partial_y = forward_rows(gathered_fwd, gates_f, weight_gu, weight_dn, capacity)
    partial_y, parts_dh[0], far[1] = lax.optimization_barrier((partial_y, parts_dh[0], far[1]))
    y_fwd = lax.psum_scatter(
        partial_y.reshape(group_count * token_count, model_width),
        "expert",
        scatter_dimension=0,
        tiled=True,
    )

    dh_sum = jnp.concatenate([jnp.sum(part.astype(jnp.float32), axis=0) for part in parts_dh])
    bwd_hat, bwd_scale = normalize(x_bwd)
    scaled_dh = norm_gain * dh_sum
    dx_bwd = (
        bwd_scale * (scaled_dh - bwd_hat * jnp.mean(bwd_hat * scaled_dh, axis=-1, keepdims=True))
    ).astype(jnp.bfloat16)

    dx_bwd, far[2] = lax.optimization_barrier((dx_bwd, far[2]))
    gradients = weight_gradients(
        which, (keep_c, keep_h, keep_hidden, keep_d), far[:2], weight_gu, weight_dn
    )
    out_gu, out_dn = weight_gradients(which, gradients, far[2:], weight_gu, weight_dn)
    return (y_fwd, dx_bwd, out_gu[None, None], out_dn[None, None])


def solution(mesh):
    rows = P(("pipe", "expert"), None)
    experts = P("pipe", "expert", None, None)
    return jax.shard_map(
        per_device,
        mesh=mesh,
        in_specs=(rows,) * 7 + (P(), experts, experts),
        out_specs=(rows, rows, experts, experts),
        check_vma=False,
    )
```
